128 devices in a mesh: dp: 4 (over y), context: 16 (over x, z), head: 2 (over core).
Axes of the slice: x: 4, y: 4, z: 4, core: 2. Of those that a mesh axis runs over, the one named last changes fastest.
Arguments:
- long_q: bfloat16 [4, 1024, 4096], P('dp', 'context', 'head'), may hold values from -5 to 5
- long_k: bfloat16 [4, 1024, 512], P('dp', 'context', 'head'), may hold values from -5 to 5
- long_v: bfloat16 [4, 1024, 512], P('dp', 'context', 'head'), may hold values from -6 to 6
- long_dout: bfloat16 [4, 1024, 4096], P('dp', 'context', 'head'), may hold values from -6 to 6
- short_q: bfloat16 [4, 2048, 4096], P('dp', 'context', 'head'), may hold values from -5 to 5
- short_k: bfloat16 [4, 2048, 512], P('dp', 'context', 'head'), may hold values from -5 to 5
- short_v: bfloat16 [4, 2048, 512], P('dp', 'context', 'head'), may hold values from -6 to 6
- short_dout: bfloat16 [4, 2048, 4096], P('dp', 'context', 'head'), may hold values from -6 to 6
- short_lengths: int32 [4, 16, 7], P('dp', 'context'), may hold values from 1 to 32, as said below
Outputs:
- long_dq: bfloat16 [4, 1024, 4096], P('dp', 'context', 'head')
- long_dk: bfloat16 [4, 1024, 512], P('dp', 'context', 'head')
- long_dv: bfloat16 [4, 1024, 512], P('dp', 'context', 'head')
- short_dq: bfloat16 [4, 2048, 4096], P('dp', 'context', 'head')
- short_dk: bfloat16 [4, 2048, 512], P('dp', 'context', 'head')
- short_dv: bfloat16 [4, 2048, 512], P('dp', 'context', 'head')
The draws below stay inside these ranges and needn't reach their ends.
Inputs may be any that keep to these rules, and one draw needn't show every extreme that they name: `short_lengths`: every block of 128 short tokens holds 7 documents whose lengths sum to 128: the first is 32 long, and the second and third, the fourth and fifth, the sixth and seventh each sum to 32.
All inputs are finite; a program needn't handle non-finite values.
Results may differ from the reference program's by a relative error of at most 0.018.
Values may be sent and summed in bfloat16 or wider, within the bound.
A program may use at most 64 MiB of HBM per device.

```python
import math
import jax
import jax.numpy as jnp
from jax import lax

HEAD = 128
Q_HEADS = 32
KV_HEADS = 4
LONG_DEV = 64
SHORT_DEV = 128
DOCS = 7
SHORT_MOST = 32
BATCHES = 4
LONG_LEN = 1024
SHORT_LEN = 2048
N_CONTEXT = 16


def rough_field(key, row_count, head_count, low_scale, high_scale):
    noise_field = jax.random.normal(key, (BATCHES, row_count, head_count, HEAD), jnp.float32)
    spread = jnp.exp(jax.random.uniform(jax.random.fold_in(key, 5), (BATCHES, row_count, head_count, 1), jnp.float32, math.log(low_scale), math.log(high_scale)))
    return jnp.clip(noise_field * spread, -5.0, 5.0)


def draw_long_q(key, part):
    key = jax.random.fold_in(key, 1)
    result_field = rough_field(key, LONG_LEN, Q_HEADS, 0.4, 2.0)
    return result_field.reshape(BATCHES, LONG_LEN, Q_HEADS * HEAD).astype(jnp.bfloat16)


def draw_long_k(key, part):
    key = jax.random.fold_in(key, 2)
    result_field = rough_field(key, LONG_LEN, KV_HEADS, 0.4, 2.0)
    return result_field.reshape(BATCHES, LONG_LEN, KV_HEADS * HEAD).astype(jnp.bfloat16)


def draw_short_q(key, part):
    key = jax.random.fold_in(key, 3)
    result_field = rough_field(key, SHORT_LEN, Q_HEADS, 0.4, 2.0)
    return result_field.reshape(BATCHES, SHORT_LEN, Q_HEADS * HEAD).astype(jnp.bfloat16)


def draw_short_k(key, part):
    key = jax.random.fold_in(key, 4)
    result_field = rough_field(key, SHORT_LEN, KV_HEADS, 0.4, 2.0)
    return result_field.reshape(BATCHES, SHORT_LEN, KV_HEADS * HEAD).astype(jnp.bfloat16)


def draw_short_lengths(key, part):
    key = jax.random.fold_in(key, 7)
    pieces = jax.random.randint(key, (BATCHES, N_CONTEXT, 3), 1, SHORT_MOST, dtype=jnp.int32)
    first_doc = jnp.full((BATCHES, N_CONTEXT, 1), SHORT_MOST, jnp.int32)
    later_docs = jnp.stack([pieces, SHORT_MOST - pieces], axis=-1).reshape(BATCHES, N_CONTEXT, 6)
    return jnp.concatenate([first_doc, later_docs], axis=-1).astype(jnp.int32)


def steps_of(key, dims, cuts, low, high):
    def one(dim, blocks):
        draws = jax.random.uniform(jax.random.fold_in(jax.random.fold_in(key, 6), dim), (blocks,), jnp.float32, low / len(cuts), high / len(cuts))
        return jnp.repeat(jnp.exp(draws), dims[dim] // blocks).reshape((-1,) + (1,) * (len(dims) - dim - 1))

    gain = one(*cuts[0])
    for cut in cuts[1:]:
        gain = gain * one(*cut)
    return gain


def bell_draw(rng, dims, width, reach, cuts=(), kind=jnp.bfloat16):
    drawn = jax.random.normal(rng, dims, jnp.float32) * width
    if len(cuts) > 0:
        drawn = steps_of(rng, dims, cuts, -0.22, 0.18) * drawn
    return jnp.clip(drawn, min=-reach, max=reach).astype(kind)


def setup_inputs(seed: int = 0) -> dict:
    key_list = jax.random.split(jax.random.key(seed), 10)
    long_q = draw_long_q(jax.random.fold_in(key_list[9], 71), 0)
    long_k = draw_long_k(jax.random.fold_in(key_list[9], 71), 0)
    long_v = bell_draw(key_list[2], (BATCHES, LONG_LEN, KV_HEADS * HEAD), 1.0, 6.0, ((0, 4), (1, 16), (2, 2)))
    long_dout = bell_draw(key_list[3], (BATCHES, LONG_LEN, Q_HEADS * HEAD), 1.0, 6.0, ((0, 4), (1, 16), (2, 2)))
    short_q = draw_short_q(jax.random.fold_in(key_list[9], 71), 0)
    short_k = draw_short_k(jax.random.fold_in(key_list[9], 71), 0)
    short_v = bell_draw(key_list[6], (BATCHES, SHORT_LEN, KV_HEADS * HEAD), 1.0, 6.0, ((0, 4), (1, 16), (2, 2)))
    short_dout = bell_draw(key_list[7], (BATCHES, SHORT_LEN, Q_HEADS * HEAD), 1.0, 6.0, ((0, 4), (1, 16), (2, 2)))
    short_lengths = draw_short_lengths(jax.random.fold_in(key_list[9], 71), 0)
    return {"long_q": long_q, "long_k": long_k, "long_v": long_v, "long_dout": long_dout, "short_q": short_q, "short_k": short_k, "short_v": short_v, "short_dout": short_dout, "short_lengths": short_lengths}


def group_grads(queries, key_rows, value_rows, grad_out, allowed, scaling):
    highest = lax.Precision.HIGHEST
    query_f = queries.astype(jnp.float32)
    key_f = key_rows.astype(jnp.float32)
    value_f = value_rows.astype(jnp.float32)
    grad_f = grad_out.astype(jnp.float32)
    score = jnp.einsum('rgd,pd->grp', query_f, key_f, precision=highest) * scaling
    score = jnp.where(allowed[None], score, -1e+30)
    row_top = lax.optimization_barrier(jnp.max(score, axis=-1, keepdims=True))
    log_total = row_top + jnp.log(lax.optimization_barrier(jnp.sum(jnp.exp(score - row_top), axis=-1, keepdims=True)))
    attn_prob = jnp.exp(score - log_total)
    grad_prob = jnp.einsum('rgd,pd->grp', grad_f, value_f, precision=highest)
    row_delta = lax.optimization_barrier(jnp.sum(attn_prob * grad_prob, axis=-1, keepdims=True))
    grad_score = (attn_prob * (grad_prob - row_delta)).astype(jnp.bfloat16)
    weights = attn_prob.astype(jnp.bfloat16)
    grad_score = lax.optimization_barrier(grad_score).astype(jnp.float32)
    weights = lax.optimization_barrier(weights).astype(jnp.float32)
    dquery = jnp.einsum('grp,pd->rgd', grad_score, key_f, precision=highest) * scaling
    dkey = jnp.einsum('grp,rgd->pd', grad_score, query_f, precision=highest) * scaling
    dvalue = jnp.einsum('grp,rgd->pd', weights, grad_f, precision=highest)
    return (dquery, dkey, dvalue)

def allowed_from(doc_lengths, row_count):
    doc_ends = jnp.cumsum(doc_lengths)
    position = jnp.arange(row_count, dtype=jnp.int32)
    doc_index = lax.optimization_barrier(jnp.sum(position[:, None] >= doc_ends[None, :], axis=1))
    same_doc = doc_index[:, None] == doc_index[None, :]
    return same_doc & (position[None, :] <= position[:, None])

def split_queries(array, count, row_count, group_size):
    shaped = array.reshape(count, row_count, KV_HEADS, group_size, HEAD)
    return shaped.transpose(0, 2, 1, 3, 4).reshape(count * KV_HEADS, row_count, group_size, HEAD)

def split_keys(array, count, row_count):
    shaped = array.reshape(count, row_count, KV_HEADS, HEAD)
    return shaped.transpose(0, 2, 1, 3).reshape(count * KV_HEADS, row_count, HEAD)

def join_queries(array, count, row_count, group_size):
    shaped = array.reshape(count, KV_HEADS, row_count, group_size, HEAD)
    return shaped.transpose(0, 2, 1, 3, 4).reshape(count, row_count, Q_HEADS * HEAD)

def join_keys(array, count, row_count):
    shaped = array.reshape(count, KV_HEADS, row_count, HEAD)
    return shaped.transpose(0, 2, 1, 3).reshape(count, row_count, KV_HEADS * HEAD)

def reference(long_q, long_k, long_v, long_dout, short_q, short_k, short_v, short_dout, short_lengths):
    group_size = Q_HEADS // KV_HEADS
    scaling = 1.0 / math.sqrt(HEAD)
    key_pos = jnp.arange(LONG_LEN, dtype=jnp.int32)

    def long_item(packed):
        query_all, key_all, value_all, grad_all = packed
        query_blocks = query_all.reshape(N_CONTEXT, LONG_DEV, group_size, HEAD)
        grad_blocks = grad_all.reshape(N_CONTEXT, LONG_DEV, group_size, HEAD)

        def block_step(carry, item):
            query_block, grad_block, block_index = item
            query_pos = block_index * LONG_DEV + jnp.arange(LONG_DEV, dtype=jnp.int32)
            allowed = key_pos[None, :] <= query_pos[:, None]
            dquery, dkey, dvalue = group_grads(query_block, key_all, value_all, grad_block, allowed, scaling)
            return ((carry[0] + dkey, carry[1] + dvalue), dquery)
        zero_rows = jnp.zeros((LONG_LEN, HEAD), jnp.float32)
        totals, dquery = lax.scan(block_step, (zero_rows, zero_rows), (query_blocks, grad_blocks, jnp.arange(N_CONTEXT, dtype=jnp.int32)))
        return (dquery.reshape(LONG_LEN, group_size, HEAD), totals[0], totals[1])
    long_items = (split_queries(long_q, BATCHES, LONG_LEN, group_size), split_keys(long_k, BATCHES, LONG_LEN), split_keys(long_v, BATCHES, LONG_LEN), split_queries(long_dout, BATCHES, LONG_LEN, group_size))
    dquery, dkey, dvalue = lax.map(long_item, long_items)
    long_dq = join_queries(dquery, BATCHES, LONG_LEN, group_size).astype(jnp.bfloat16)
    long_dk = join_keys(dkey, BATCHES, LONG_LEN).astype(jnp.bfloat16)
    long_dv = join_keys(dvalue, BATCHES, LONG_LEN).astype(jnp.bfloat16)
    block_count = BATCHES * N_CONTEXT
    doc_lengths = jnp.repeat(short_lengths.reshape(block_count, DOCS), KV_HEADS, axis=0)

    def short_item(packed):
        allowed = allowed_from(packed[4], SHORT_DEV)
        return group_grads(packed[0], packed[1], packed[2], packed[3], allowed, scaling)
    short_items = (split_queries(short_q.reshape(block_count, SHORT_DEV, Q_HEADS * HEAD), block_count, SHORT_DEV, group_size), split_keys(short_k.reshape(block_count, SHORT_DEV, KV_HEADS * HEAD), block_count, SHORT_DEV), split_keys(short_v.reshape(block_count, SHORT_DEV, KV_HEADS * HEAD), block_count, SHORT_DEV), split_queries(short_dout.reshape(block_count, SHORT_DEV, Q_HEADS * HEAD), block_count, SHORT_DEV, group_size), doc_lengths)
    dquery, dkey, dvalue = lax.map(short_item, short_items)
    short_dq = join_queries(dquery, block_count, SHORT_DEV, group_size).reshape(BATCHES, SHORT_LEN, Q_HEADS * HEAD)
    short_dk = join_keys(dkey, block_count, SHORT_DEV).reshape(BATCHES, SHORT_LEN, KV_HEADS * HEAD)
    short_dv = join_keys(dvalue, block_count, SHORT_DEV).reshape(BATCHES, SHORT_LEN, KV_HEADS * HEAD)
    return (long_dq, long_dk, long_dv, short_dq.astype(jnp.bfloat16), short_dk.astype(jnp.bfloat16), short_dv.astype(jnp.bfloat16))
```

```python
import math

import jax
import jax.numpy as jnp
from jax import lax
from jax.experimental import pallas as pl
from jax.experimental.pallas import tpu as pltpu
from jax.sharding import PartitionSpec as P

HEAD = 128
KV = 2
GROUP = 8
LONG = 64
SHORT = 128
SEG = 32
DOCS = 7
N = 16
PER = 4
CHUNK = PER * LONG
ROWS = GROUP * LONG
MESH = pl.DeviceIdType.MESH
SCALE = 1.0 / math.sqrt(HEAD)
SCALE2 = SCALE * math.log2(math.e)
NEG = -1e30
NT = (((1,), (1,)), ((), ()))
TN = (((0,), (0,)), ((), ()))


def nt(a, b):
    return lax.dot_general(a, b, NT, preferred_element_type=jnp.float32)


def tn(a, b):
    return lax.dot_general(a, b, TN, preferred_element_type=jnp.float32)


def nn(a, b):
    return jnp.dot(a, b, preferred_element_type=jnp.float32)


def kernel(
    lq,
    lk,
    lv,
    ldo,
    sq,
    sk,
    sv,
    sdo,
    lens,
    o_lq,
    o_lk,
    o_lv,
    o_sq,
    o_sk,
    o_sv,
    q_in,
    do_in,
    sq_in,
    sk_in,
    sv_in,
    sdo_in,
    q_s,
    do_s,
    k_all,
    v_all,
    e_s,
    gp_s,
    gs_s,
    m_s,
    l_s,
    d_s,
    dv_out,
    dk_out,
    dv_in,
    dk_in,
    dq_o,
    dk_o,
    dv_o,
    sdq_o,
    sdk_o,
    sdv_o,
    in_sem,
    out_sem,
    k_send,
    k_recv,
    v_send,
    v_recv,
    dv_send,
    dv_recv,
    dk_send,
    dk_recv,
):
    me = lax.axis_index("context")
    dp = lax.axis_index("dp")
    hd = lax.axis_index("head")
    row = me // PER
    col = me % PER

    def dev(j):
        return (dp, j, hd)

    barrier = pltpu.get_barrier_semaphore()
    for d in range(1, N):
        pl.semaphore_signal(
            barrier, inc=1, device_id=dev(lax.rem(me + d, N)), device_id_type=MESH
        )

    loads = [
        pltpu.make_async_copy(src, dst, in_sem.at[i])
        for i, (src, dst) in enumerate(
            (
                (lk, k_all.at[me]),
                (lv, v_all.at[me]),
                (sq, sq_in),
                (sk, sk_in),
                (sdo, sdo_in),
                (sv, sv_in),
                (lq, q_in),
                (ldo, do_in),
            )
        )
    ]
    for b in range(PER):

        @pl.when(b > col)
        def _():
            k_all[row * PER + b] = jnp.zeros((LONG, KV * HEAD), jnp.bfloat16)
            v_all[row * PER + b] = jnp.zeros((LONG, KV * HEAD), jnp.bfloat16)

    for load in loads:
        load.start()
    pl.semaphore_wait(barrier, N - 1)

    def k_copy(j, slot):
        return pltpu.make_async_remote_copy(
            lk, k_all.at[slot], k_send.at[j], k_recv.at[slot], dev(j), MESH
        )

    def v_copy(j, slot):
        return pltpu.make_async_remote_copy(
            lv, v_all.at[slot], v_send.at[j], v_recv.at[slot], dev(j), MESH
        )

    def dv_copy(j, slot):
        return pltpu.make_async_remote_copy(
            dv_out.at[j], dv_in.at[slot], dv_send.at[j], dv_recv.at[slot], dev(j), MESH
        )

    def dk_copy(j, slot):
        return pltpu.make_async_remote_copy(
            dk_out.at[j], dk_in.at[slot], dk_send.at[j], dk_recv.at[slot], dev(j), MESH
        )

    def send_k(i, _):
        k_copy(N - 1 - i, me).start()
        return 0

    def send_v(i, _):
        v_copy(N - 1 - i, me).start()
        return 0

    lax.fori_loop(0, N - 1 - me, send_k, 0)
    lax.fori_loop(0, N - 1 - me, send_v, 0)

    for i in (2, 3, 4, 5):
        loads[i].wait()
    ends = []
    total = jnp.int32(0)
    for i in range(DOCS):
        total = total + lens[0, 0, i]
        ends.append(total)
    outs = []
    for seg in range(SHORT // SEG):
        base = seg * SEG
        key_pos = base + lax.broadcasted_iota(jnp.int32, (SEG, GROUP * SEG), 0)
        query_pos = base + lax.rem(
            lax.broadcasted_iota(jnp.int32, (SEG, GROUP * SEG), 1), SEG
        )
        key_doc = jnp.zeros((SEG, GROUP * SEG), jnp.int32)
        query_doc = jnp.zeros((SEG, GROUP * SEG), jnp.int32)
        for end in ends:
            key_doc = key_doc + (key_pos >= end).astype(jnp.int32)
            query_doc = query_doc + (query_pos >= end).astype(jnp.int32)
        allowed = (key_doc == query_doc) & (key_pos <= query_pos)
        rows = slice(base, base + SEG)
        for h in range(KV):
            kv = slice(h * HEAD, (h + 1) * HEAD)
            cols = [
                slice((h * GROUP + g) * HEAD, (h * GROUP + g + 1) * HEAD)
                for g in range(GROUP)
            ]
            q = jnp.concatenate([sq_in[rows, c] for c in cols], axis=0)
            do = jnp.concatenate([sdo_in[rows, c] for c in cols], axis=0)
            k = sk_in[rows, kv]
            v = sv_in[rows, kv]
            s = jnp.where(allowed, nt(k, q), NEG)
            e = jnp.exp2((s - jnp.max(s, axis=0, keepdims=True)) * SCALE2)
            p = e * (1.0 / jnp.sum(e, axis=0, keepdims=True))
            gp = nt(v, do)
            delta = jnp.sum(p * gp, axis=0, keepdims=True)
            gs = (p * (gp - delta)).astype(jnp.bfloat16)
            sdv_o[rows, kv] = nn(p.astype(jnp.bfloat16), do).astype(jnp.bfloat16)
            sdk_o[rows, kv] = (nn(gs, q) * SCALE).astype(jnp.bfloat16)
            dq = (tn(gs, k) * SCALE).astype(jnp.bfloat16)
            for g, c in enumerate(cols):
                sdq_o[rows, c] = dq[g * SEG : (g + 1) * SEG]
    short_stores = [
        pltpu.make_async_copy(src, dst, out_sem.at[i])
        for i, (src, dst) in enumerate(((sdq_o, o_sq), (sdk_o, o_sk), (sdv_o, o_sv)))
    ]
    for store in short_stores:
        store.start()

    for i in (6, 7, 0, 1):
        loads[i].wait()
    for h in range(KV):
        for g in range(GROUP):
            c = slice((h * GROUP + g) * HEAD, (h * GROUP + g + 1) * HEAD)
            q_s[h, g * LONG : (g + 1) * LONG] = q_in[:, c]
            do_s[h, g * LONG : (g + 1) * LONG] = do_in[:, c]

    def keys_of(ref, c, h):
        part = ref[pl.ds(c * PER, PER), :, h * HEAD : (h + 1) * HEAD]
        return part.reshape(CHUNK, HEAD)

    def scores(c, causal):
        for h in range(KV):
            s = nt(keys_of(k_all, c, h), q_s[h])
            if causal is not None:
                s = jnp.where(causal, s, NEG)
            m = jnp.max(s, axis=0, keepdims=True)
            e = jnp.exp2((s - m) * SCALE2)
            e_s[h, c] = e
            m_s[h, c] = m
            l_s[h, c] = jnp.sum(e, axis=0, keepdims=True)

    def score_step(c, _):
        for b in range(PER):
            k_copy(me, c * PER + b).wait_recv()
        scores(c, None)
        return 0

    lax.fori_loop(0, row, score_step, 0)

    def wait_k(b, _):
        k_copy(me, row * PER + b).wait_recv()
        return 0

    lax.fori_loop(0, col, wait_k, 0)
    key_pos = lax.broadcasted_iota(jnp.int32, (CHUNK, ROWS), 0)
    query_pos = lax.rem(lax.broadcasted_iota(jnp.int32, (CHUNK, ROWS), 1), LONG)
    scores(row, key_pos <= query_pos + col * LONG)

    for h in range(KV):
        top = lax.fori_loop(
            0, row, lambda c, t: jnp.maximum(t, m_s[h, c]), m_s[h, row]
        )
        sums = lax.fori_loop(
            0,
            row + 1,
            lambda c, t: t + l_s[h, c] * jnp.exp2((m_s[h, c] - top) * SCALE2),
            jnp.zeros((1, ROWS), jnp.float32),
        )
        inverse = 1.0 / sums

        def weigh(c, _):
            m_s[h, c] = jnp.exp2((m_s[h, c] - top) * SCALE2) * inverse
            return 0

        lax.fori_loop(0, row + 1, weigh, 0)

    def value_grads(c):
        for h in range(KV):
            p = e_s[h, c] * m_s[h, c]
            e_s[h, c] = p
            dv = nn(p.astype(jnp.bfloat16), do_s[h])
            dv_out[pl.ds(c * PER, PER), :, h * HEAD : (h + 1) * HEAD] = dv.astype(
                jnp.bfloat16
            ).reshape(PER, LONG, HEAD)

    def value_step(c, _):
        value_grads(c)
        for b in range(PER):
            dv_copy(c * PER + b, me).start()
        return 0

    lax.fori_loop(0, row, value_step, 0)
    value_grads(row)

    def send_dv(b, _):
        dv_copy(row * PER + b, me).start()
        return 0

    lax.fori_loop(0, col, send_dv, 0)

    def prob_grads(c):
        for h in range(KV):
            gp = nt(keys_of(v_all, c, h), do_s[h])
            gp_s[h, c] = gp
            d_s[h] += jnp.sum(e_s[h, c] * gp, axis=0, keepdims=True)

    d_s[...] = jnp.zeros_like(d_s)

    def prob_step(c, _):
        for b in range(PER):
            v_copy(me, c * PER + b).wait_recv()
        prob_grads(c)
        return 0

    lax.fori_loop(0, row, prob_step, 0)

    def wait_v(b, _):
        v_copy(me, row * PER + b).wait_recv()
        return 0

    lax.fori_loop(0, col, wait_v, 0)
    prob_grads(row)

    def key_grads(c):
        for h in range(KV):
            gs = (e_s[h, c] * (gp_s[h, c] - d_s[h])).astype(jnp.bfloat16)
            gs_s[h, c] = gs
            dk = nn(gs, q_s[h]) * SCALE
            dk_out[pl.ds(c * PER, PER), :, h * HEAD : (h + 1) * HEAD] = dk.astype(
                jnp.bfloat16
            ).reshape(PER, LONG, HEAD)

    def key_step(c, _):
        key_grads(c)
        for b in range(PER):
            dk_copy(c * PER + b, me).start()
        return 0

    lax.fori_loop(0, row, key_step, 0)
    key_grads(row)

    def send_dk(b, _):
        dk_copy(row * PER + b, me).start()
        return 0

    lax.fori_loop(0, col, send_dk, 0)

    for h in range(KV):
        dq = lax.fori_loop(
            0,
            row + 1,
            lambda c, t: t + tn(gs_s[h, c], keys_of(k_all, c, h)),
            jnp.zeros((ROWS, HEAD), jnp.float32),
        )
        dq = (dq * SCALE).astype(jnp.bfloat16)
        for g in range(GROUP):
            c = slice((h * GROUP + g) * HEAD, (h * GROUP + g + 1) * HEAD)
            dq_o[:, c] = dq[g * LONG : (g + 1) * LONG]
    stores = [pltpu.make_async_copy(dq_o, o_lq, out_sem.at[3])]
    stores[0].start()

    def add_dv(i, t):
        j = N - 1 - i
        dv_copy(me, j).wait_recv()
        return t + dv_in[j].astype(jnp.float32)

    def add_dk(i, t):
        j = N - 1 - i
        dk_copy(me, j).wait_recv()
        return t + dk_in[j].astype(jnp.float32)

    dv = lax.fori_loop(0, N - 1 - me, add_dv, dv_out[me].astype(jnp.float32))
    dv_o[...] = dv.astype(jnp.bfloat16)
    stores.append(pltpu.make_async_copy(dv_o, o_lv, out_sem.at[4]))
    stores[1].start()
    dk = lax.fori_loop(0, N - 1 - me, add_dk, dk_out[me].astype(jnp.float32))
    dk_o[...] = dk.astype(jnp.bfloat16)
    stores.append(pltpu.make_async_copy(dk_o, o_lk, out_sem.at[5]))
    stores[2].start()

    def sent_kv(i, _):
        k_copy(N - 1 - i, me).wait_send()
        v_copy(N - 1 - i, me).wait_send()
        return 0

    def sent_grads(j, _):
        dv_copy(j, me).wait_send()
        dk_copy(j, me).wait_send()
        return 0

    lax.fori_loop(0, N - 1 - me, sent_kv, 0)
    lax.fori_loop(0, me, sent_grads, 0)
    for store in short_stores + stores:
        store.wait()


def on_device(lq, lk, lv, ldo, sq, sk, sv, sdo, lens):
    bf, f32 = jnp.bfloat16, jnp.float32
    kv, qw = KV * HEAD, KV * GROUP * HEAD
    shapes = [(LONG, qw), (LONG, kv), (LONG, kv), (SHORT, qw), (SHORT, kv), (SHORT, kv)]
    any_spec = pl.BlockSpec(memory_space=pl.ANY)
    outs = pl.pallas_call(
        kernel,
        out_shape=[jax.ShapeDtypeStruct(s, bf) for s in shapes],
        in_specs=[any_spec] * 8 + [pl.BlockSpec(memory_space=pltpu.SMEM)],
        out_specs=[any_spec] * 6,
        scratch_shapes=[
            pltpu.VMEM((LONG, qw), bf),
            pltpu.VMEM((LONG, qw), bf),
            pltpu.VMEM((SHORT, qw), bf),
            pltpu.VMEM((SHORT, kv), bf),
            pltpu.VMEM((SHORT, kv), bf),
            pltpu.VMEM((SHORT, qw), bf),
            pltpu.VMEM((KV, ROWS, HEAD), bf),
            pltpu.VMEM((KV, ROWS, HEAD), bf),
            pltpu.VMEM((N, LONG, kv), bf),
            pltpu.VMEM((N, LONG, kv), bf),
            pltpu.VMEM((KV, PER, CHUNK, ROWS), f32),
            pltpu.VMEM((KV, PER, CHUNK, ROWS), f32),
            pltpu.VMEM((KV, PER, CHUNK, ROWS), bf),
            pltpu.VMEM((KV, PER, 1, ROWS), f32),
            pltpu.VMEM((KV, PER, 1, ROWS), f32),
            pltpu.VMEM((KV, 1, ROWS), f32),
            pltpu.VMEM((N, LONG, kv), bf),
            pltpu.VMEM((N, LONG, kv), bf),
            pltpu.VMEM((N, LONG, kv), bf),
            pltpu.VMEM((N, LONG, kv), bf),
        ]
        + [pltpu.VMEM(s, bf) for s in shapes]
        + [pltpu.SemaphoreType.DMA((8,)), pltpu.SemaphoreType.DMA((6,))]
        + [pltpu.SemaphoreType.DMA((N,))] * 8,
        compiler_params=pltpu.CompilerParams(
            collective_id=0, has_side_effects=True, vmem_limit_bytes=40 << 20
        ),
        name="attention_grads",
    )(lq[0], lk[0], lv[0], ldo[0], sq[0], sk[0], sv[0], sdo[0], lens)
    return tuple(o[None] for o in outs)


def solution(mesh):
    spec = P("dp", "context", "head")
    return jax.shard_map(
        on_device,
        mesh=mesh,
        in_specs=(spec,) * 8 + (P("dp", "context", None),),
        out_specs=(spec,) * 6,
        check_vma=False,
    )
```

```python
import math

import jax
import jax.numpy as jnp
from jax import lax
from jax.experimental import pallas as pl
from jax.experimental.pallas import tpu as pltpu
from jax.sharding import PartitionSpec as P

HEAD = 128
KV = 2
GROUP = 8
LONG = 64
SHORT = 128
SEG = 32
DOCS = 7
N = 16
PER = 4
CHUNK = PER * LONG
ROWS = GROUP * LONG
MESH = pl.DeviceIdType.MESH
SCALE = 1.0 / math.sqrt(HEAD)
SCALE2 = SCALE * math.log2(math.e)
NEG = -1e30
NT = (((1,), (1,)), ((), ()))
TN = (((0,), (0,)), ((), ()))


def nt(a, b):
    return lax.dot_general(a, b, NT, preferred_element_type=jnp.float32)


def tn(a, b):
    return lax.dot_general(a, b, TN, preferred_element_type=jnp.float32)


def nn(a, b):
    return jnp.dot(a, b, preferred_element_type=jnp.float32)


def kernel(
    lq,
    lk,
    lv,
    ldo,
    sq,
    sk,
    sv,
    sdo,
    lens_hbm,
    dq_o,
    dk_o,
    dv_o,
    sdq_o,
    sdk_o,
    sdv_o,
    q_in,
    do_in,
    sq_in,
    sk_in,
    sv_in,
    sdo_in,
    q_s,
    do_s,
    k_all,
    v_all,
    e_s,
    gp_s,
    gs_s,
    m_s,
    l_s,
    d_s,
    dv_out,
    dk_out,
    dv_in,
    dk_in,
    lens,
    in_sem,
    k_send,
    k_recv,
    v_send,
    v_recv,
    dv_send,
    dv_recv,
    dk_send,
    dk_recv,
):
    me = lax.axis_index("context")
    dp = lax.axis_index("dp")
    hd = lax.axis_index("head")
    row = me // PER
    col = me % PER

    def dev(j):
        return (dp, j, hd)

    barrier = pltpu.get_barrier_semaphore()
    for d in range(1, N):
        pl.semaphore_signal(
            barrier, inc=1, device_id=dev(lax.rem(me + d, N)), device_id_type=MESH
        )

    loads = [
        pltpu.make_async_copy(src, dst, in_sem.at[i])
        for i, (src, dst) in enumerate(
            (
                (lk, k_all.at[me]),
                (lv, v_all.at[me]),
                (sq, sq_in),
                (sk, sk_in),
                (sdo, sdo_in),
                (sv, sv_in),
                (lq, q_in),
                (ldo, do_in),
                (lens_hbm, lens),
            )
        )
    ]
    for b in range(PER):

        @pl.when(b > col)
        def _():
            k_all[row * PER + b] = jnp.zeros((LONG, KV * HEAD), jnp.bfloat16)
            v_all[row * PER + b] = jnp.zeros((LONG, KV * HEAD), jnp.bfloat16)

    for load in loads:
        load.start()
    pl.semaphore_wait(barrier, N - 1)

    def k_copy(j, slot):
        return pltpu.make_async_remote_copy(
            lk, k_all.at[slot], k_send.at[j], k_recv.at[slot], dev(j), MESH
        )

    def v_copy(j, slot):
        return pltpu.make_async_remote_copy(
            lv, v_all.at[slot], v_send.at[j], v_recv.at[slot], dev(j), MESH
        )

    def dv_copy(j, slot):
        return pltpu.make_async_remote_copy(
            dv_out.at[j], dv_in.at[slot], dv_send.at[j], dv_recv.at[slot], dev(j), MESH
        )

    def dk_copy(j, slot):
        return pltpu.make_async_remote_copy(
            dk_out.at[j], dk_in.at[slot], dk_send.at[j], dk_recv.at[slot], dev(j), MESH
        )

    def send_k(i, _):
        k_copy(N - 1 - i, me).start()
        return 0

    def send_v(i, _):
        v_copy(N - 1 - i, me).start()
        return 0

    lax.fori_loop(0, N - 1 - me, send_k, 0)
    lax.fori_loop(0, N - 1 - me, send_v, 0)

    for i in (2, 3, 4, 5, 8):
        loads[i].wait()
    ends = []
    total = jnp.int32(0)
    for i in range(DOCS):
        total = total + lens[0, 0, i]
        ends.append(total)
    outs = []
    for seg in range(SHORT // SEG):
        base = seg * SEG
        key_pos = base + lax.broadcasted_iota(jnp.int32, (SEG, GROUP * SEG), 0)
        query_pos = base + lax.rem(
            lax.broadcasted_iota(jnp.int32, (SEG, GROUP * SEG), 1), SEG
        )
        key_doc = jnp.zeros((SEG, GROUP * SEG), jnp.int32)
        query_doc = jnp.zeros((SEG, GROUP * SEG), jnp.int32)
        for end in ends:
            key_doc = key_doc + (key_pos >= end).astype(jnp.int32)
            query_doc = query_doc + (query_pos >= end).astype(jnp.int32)
        allowed = (key_doc == query_doc) & (key_pos <= query_pos)
        rows = slice(base, base + SEG)
        for h in range(KV):
            kv = slice(h * HEAD, (h + 1) * HEAD)
            cols = [
                slice((h * GROUP + g) * HEAD, (h * GROUP + g + 1) * HEAD)
                for g in range(GROUP)
            ]
            q = jnp.concatenate([sq_in[rows, c] for c in cols], axis=0)
            do = jnp.concatenate([sdo_in[rows, c] for c in cols], axis=0)
            k = sk_in[rows, kv]
            v = sv_in[rows, kv]
            s = jnp.where(allowed, nt(k, q), NEG)
            e = jnp.exp2((s - jnp.max(s, axis=0, keepdims=True)) * SCALE2)
            p = e * (1.0 / jnp.sum(e, axis=0, keepdims=True))
            gp = nt(v, do)
            delta = jnp.sum(p * gp, axis=0, keepdims=True)
            gs = (p * (gp - delta)).astype(jnp.bfloat16)
            sdv_o[rows, kv] = nn(p.astype(jnp.bfloat16), do).astype(jnp.bfloat16)
            sdk_o[rows, kv] = (nn(gs, q) * SCALE).astype(jnp.bfloat16)
            dq = (tn(gs, k) * SCALE).astype(jnp.bfloat16)
            for g, c in enumerate(cols):
                sdq_o[rows, c] = dq[g * SEG : (g + 1) * SEG]

    for i in (6, 7, 0, 1):
        loads[i].wait()
    for h in range(KV):
        for g in range(GROUP):
            c = slice((h * GROUP + g) * HEAD, (h * GROUP + g + 1) * HEAD)
            q_s[h, g * LONG : (g + 1) * LONG] = q_in[:, c]
            do_s[h, g * LONG : (g + 1) * LONG] = do_in[:, c]

    def keys_of(ref, c, h):
        part = ref[pl.ds(c * PER, PER), :, h * HEAD : (h + 1) * HEAD]
        return part.reshape(CHUNK, HEAD)

    def scores(c, causal):
        for h in range(KV):
            s = nt(keys_of(k_all, c, h), q_s[h])
            if causal is not None:
                s = jnp.where(causal, s, NEG)
            m = jnp.max(s, axis=0, keepdims=True)
            e = jnp.exp2((s - m) * SCALE2)
            e_s[h, c] = e
            m_s[h, c] = m
            l_s[h, c] = jnp.sum(e, axis=0, keepdims=True)

    def score_step(c, _):
        for b in range(PER):
            k_copy(me, c * PER + b).wait_recv()
        scores(c, None)
        return 0

    lax.fori_loop(0, row, score_step, 0)

    def wait_k(b, _):
        k_copy(me, row * PER + b).wait_recv()
        return 0

    lax.fori_loop(0, col, wait_k, 0)
    key_pos = lax.broadcasted_iota(jnp.int32, (CHUNK, ROWS), 0)
    query_pos = lax.rem(lax.broadcasted_iota(jnp.int32, (CHUNK, ROWS), 1), LONG)
    scores(row, key_pos <= query_pos + col * LONG)

    for h in range(KV):
        top = lax.fori_loop(
            0, row, lambda c, t: jnp.maximum(t, m_s[h, c]), m_s[h, row]
        )
        sums = lax.fori_loop(
            0,
            row + 1,
            lambda c, t: t + l_s[h, c] * jnp.exp2((m_s[h, c] - top) * SCALE2),
            jnp.zeros((1, ROWS), jnp.float32),
        )
        inverse = 1.0 / sums

        def weigh(c, _):
            m_s[h, c] = jnp.exp2((m_s[h, c] - top) * SCALE2) * inverse
            return 0

        lax.fori_loop(0, row + 1, weigh, 0)

    def value_grads(c):
        for h in range(KV):
            p = e_s[h, c] * m_s[h, c]
            e_s[h, c] = p
            dv = nn(p.astype(jnp.bfloat16), do_s[h])
            dv_out[pl.ds(c * PER, PER), :, h * HEAD : (h + 1) * HEAD] = dv.astype(
                jnp.bfloat16
            ).reshape(PER, LONG, HEAD)

    def value_step(c, _):
        value_grads(c)
        for b in range(PER):
            dv_copy(c * PER + b, me).start()
        return 0

    lax.fori_loop(0, row, value_step, 0)
    value_grads(row)

    def send_dv(b, _):
        dv_copy(row * PER + b, me).start()
        return 0

    lax.fori_loop(0, col, send_dv, 0)

    def prob_grads(c):
        for h in range(KV):
            gp = nt(keys_of(v_all, c, h), do_s[h])
            gp_s[h, c] = gp
            d_s[h] += jnp.sum(e_s[h, c] * gp, axis=0, keepdims=True)

    d_s[...] = jnp.zeros_like(d_s)

    def prob_step(c, _):
        for b in range(PER):
            v_copy(me, c * PER + b).wait_recv()
        prob_grads(c)
        return 0

    lax.fori_loop(0, row, prob_step, 0)

    def wait_v(b, _):
        v_copy(me, row * PER + b).wait_recv()
        return 0

    lax.fori_loop(0, col, wait_v, 0)
    prob_grads(row)

    def key_grads(c):
        for h in range(KV):
            gs = (e_s[h, c] * (gp_s[h, c] - d_s[h])).astype(jnp.bfloat16)
            gs_s[h, c] = gs
            dk = nn(gs, q_s[h]) * SCALE
            dk_out[pl.ds(c * PER, PER), :, h * HEAD : (h + 1) * HEAD] = dk.astype(
                jnp.bfloat16
            ).reshape(PER, LONG, HEAD)

    def key_step(c, _):
        key_grads(c)
        for b in range(PER):
            dk_copy(c * PER + b, me).start()
        return 0

    lax.fori_loop(0, row, key_step, 0)
    key_grads(row)

    def send_dk(b, _):
        dk_copy(row * PER + b, me).start()
        return 0

    lax.fori_loop(0, col, send_dk, 0)

    for h in range(KV):
        dq = lax.fori_loop(
            0,
            row + 1,
            lambda c, t: t + tn(gs_s[h, c], keys_of(k_all, c, h)),
            jnp.zeros((ROWS, HEAD), jnp.float32),
        )
        dq = (dq * SCALE).astype(jnp.bfloat16)
        for g in range(GROUP):
            c = slice((h * GROUP + g) * HEAD, (h * GROUP + g + 1) * HEAD)
            dq_o[:, c] = dq[g * LONG : (g + 1) * LONG]

    def add_dv(i, t):
        j = N - 1 - i
        dv_copy(me, j).wait_recv()
        return t + dv_in[j].astype(jnp.float32)

    def add_dk(i, t):
        j = N - 1 - i
        dk_copy(me, j).wait_recv()
        return t + dk_in[j].astype(jnp.float32)

    dv = lax.fori_loop(0, N - 1 - me, add_dv, dv_out[me].astype(jnp.float32))
    dv_o[...] = dv.astype(jnp.bfloat16)
    dk = lax.fori_loop(0, N - 1 - me, add_dk, dk_out[me].astype(jnp.float32))
    dk_o[...] = dk.astype(jnp.bfloat16)

    def sent_kv(i, _):
        k_copy(N - 1 - i, me).wait_send()
        v_copy(N - 1 - i, me).wait_send()
        return 0

    def sent_grads(j, _):
        dv_copy(j, me).wait_send()
        dk_copy(j, me).wait_send()
        return 0

    lax.fori_loop(0, N - 1 - me, sent_kv, 0)
    lax.fori_loop(0, me, sent_grads, 0)


def write_results(*refs):
    sem = refs[12]
    copies = [pltpu.make_async_copy(refs[i], refs[6 + i], sem.at[i]) for i in range(6)]
    for copy in copies:
        copy.start()
    for copy in copies:
        copy.wait()


def on_device(lq, lk, lv, ldo, sq, sk, sv, sdo, lens):
    bf, f32 = jnp.bfloat16, jnp.float32
    args = (lq[0], lk[0], lv[0], ldo[0], sq[0], sk[0], sv[0], sdo[0], lens)
    kv, qw = KV * HEAD, KV * GROUP * HEAD
    shapes = [(LONG, qw), (LONG, kv), (LONG, kv), (SHORT, qw), (SHORT, kv), (SHORT, kv)]
    any_spec = pl.BlockSpec(memory_space=pltpu.HBM)
    vmem_spec = pl.BlockSpec(memory_space=pltpu.VMEM)
    outs = pl.pallas_call(
        kernel,
        out_shape=[pltpu.VMEM(s, bf) for s in shapes],
        in_specs=[any_spec] * 9,
        out_specs=[vmem_spec] * 6,
        scratch_shapes=[
            pltpu.VMEM((LONG, qw), bf),
            pltpu.VMEM((LONG, qw), bf),
            pltpu.VMEM((SHORT, qw), bf),
            pltpu.VMEM((SHORT, kv), bf),
            pltpu.VMEM((SHORT, kv), bf),
            pltpu.VMEM((SHORT, qw), bf),
            pltpu.VMEM((KV, ROWS, HEAD), bf),
            pltpu.VMEM((KV, ROWS, HEAD), bf),
            pltpu.VMEM((N, LONG, kv), bf),
            pltpu.VMEM((N, LONG, kv), bf),
            pltpu.VMEM((KV, PER, CHUNK, ROWS), f32),
            pltpu.VMEM((KV, PER, CHUNK, ROWS), f32),
            pltpu.VMEM((KV, PER, CHUNK, ROWS), bf),
            pltpu.VMEM((KV, PER, 1, ROWS), f32),
            pltpu.VMEM((KV, PER, 1, ROWS), f32),
            pltpu.VMEM((KV, 1, ROWS), f32),
            pltpu.VMEM((N, LONG, kv), bf),
            pltpu.VMEM((N, LONG, kv), bf),
            pltpu.VMEM((N, LONG, kv), bf),
            pltpu.VMEM((N, LONG, kv), bf),
        ]
        + [pltpu.SMEM((1, 1, DOCS), jnp.int32)]
        + [pltpu.SemaphoreType.DMA((9,))]
        + [pltpu.SemaphoreType.DMA((N,))] * 8,
        compiler_params=pltpu.CompilerParams(
            collective_id=0, has_side_effects=True, vmem_limit_bytes=40 << 20
        ),
        name="attention_grads",
    )(*(pltpu.with_memory_space_constraint(a, pltpu.HBM) for a in args))
    outs = pl.pallas_call(
        write_results,
        out_shape=[jax.ShapeDtypeStruct(s, bf) for s in shapes],
        in_specs=[vmem_spec] * 6,
        out_specs=[any_spec] * 6,
        scratch_shapes=[pltpu.SemaphoreType.DMA((6,))],
        name="write_results",
    )(*outs)
    return tuple(o[None] for o in outs)


def solution(mesh):
    spec = P("dp", "context", "head")
    return jax.shard_map(
        on_device,
        mesh=mesh,
        in_specs=(spec,) * 8 + (P("dp", "context", None),),
        out_specs=(spec,) * 6,
        check_vma=False,
    )
```

```python
import math

import jax
import jax.numpy as jnp
from jax import lax
from jax.experimental import pallas as pl
from jax.experimental.pallas import tpu as pltpu
from jax.sharding import PartitionSpec as P

HEAD = 128
KV = 2
GROUP = 8
LONG = 64
SHORT = 128
SEG = 32
DOCS = 7
N = 16
PER = 4
CHUNK = PER * LONG
ROWS = GROUP * LONG
MESH = pl.DeviceIdType.MESH
SCALE = 1.0 / math.sqrt(HEAD)
SCALE2 = SCALE * math.log2(math.e)
NEG = -1e30
NT = (((1,), (1,)), ((), ()))
TN = (((0,), (0,)), ((), ()))


def nt(a, b):
    return lax.dot_general(a, b, NT, preferred_element_type=jnp.float32)


def tn(a, b):
    return lax.dot_general(a, b, TN, preferred_element_type=jnp.float32)


def nn(a, b):
    return jnp.dot(a, b, preferred_element_type=jnp.float32)


def kernel(
    lq,
    lk,
    lv,
    ldo,
    sq,
    sk,
    sv,
    sdo,
    lens_hbm,
    dq_o,
    dk_o,
    dv_o,
    sdq_o,
    sdk_o,
    sdv_o,
    q_in,
    do_in,
    sq_in,
    sk_in,
    sv_in,
    sdo_in,
    q_s,
    do_s,
    k_all,
    v_all,
    e_s,
    gp_s,
    gs_s,
    m_s,
    l_s,
    d_s,
    dv_out,
    dk_out,
    dv_in,
    dk_in,
    lens,
    in_sem,
    k_send,
    k_recv,
    v_send,
    v_recv,
    dv_send,
    dv_recv,
    dk_send,
    dk_recv,
):
    me = lax.axis_index("context")
    dp = lax.axis_index("dp")
    hd = lax.axis_index("head")
    row = me // PER
    col = me % PER

    def dev(j):
        return (dp, j, hd)

    barrier = pltpu.get_barrier_semaphore()
    for d in range(1, N):
        pl.semaphore_signal(
            barrier, inc=1, device_id=dev(lax.rem(me + d, N)), device_id_type=MESH
        )

    loads = [
        pltpu.make_async_copy(src, dst, in_sem.at[i])
        for i, (src, dst) in enumerate(
            (
                (lk, k_all.at[me]),
                (lv, v_all.at[me]),
                (sq, sq_in),
                (sk, sk_in),
                (sdo, sdo_in),
                (sv, sv_in),
                (lq, q_in),
                (ldo, do_in),
                (lens_hbm, lens),
            )
        )
    ]
    for b in range(PER):

        @pl.when(b > col)
        def _():
            k_all[row * PER + b] = jnp.zeros((LONG, KV * HEAD), jnp.bfloat16)
            v_all[row * PER + b] = jnp.zeros((LONG, KV * HEAD), jnp.bfloat16)

    for load in loads:
        load.start()
    pl.semaphore_wait(barrier, N - 1)

    def k_copy(j, slot):
        return pltpu.make_async_remote_copy(
            lk, k_all.at[slot], k_send.at[j], k_recv.at[slot], dev(j), MESH
        )

    def v_copy(j, slot):
        return pltpu.make_async_remote_copy(
            lv, v_all.at[slot], v_send.at[j], v_recv.at[slot], dev(j), MESH
        )

    def dv_copy(j, slot):
        return pltpu.make_async_remote_copy(
            dv_out.at[j], dv_in.at[slot], dv_send.at[j], dv_recv.at[slot], dev(j), MESH
        )

    def dk_copy(j, slot):
        return pltpu.make_async_remote_copy(
            dk_out.at[j], dk_in.at[slot], dk_send.at[j], dk_recv.at[slot], dev(j), MESH
        )

    def send_k(i, _):
        k_copy(N - 1 - i, me).start()
        return 0

    def send_v(i, _):
        v_copy(N - 1 - i, me).start()
        return 0

    lax.fori_loop(0, N - 1 - me, send_k, 0)
    lax.fori_loop(0, N - 1 - me, send_v, 0)

    for i in (2, 3, 4, 5, 8):
        loads[i].wait()
    ends = []
    total = jnp.int32(0)
    for i in range(DOCS):
        total = total + lens[0, 0, i]
        ends.append(total)
    outs = []
    for seg in range(SHORT // SEG):
        base = seg * SEG
        key_pos = base + lax.broadcasted_iota(jnp.int32, (SEG, GROUP * SEG), 0)
        query_pos = base + lax.rem(
            lax.broadcasted_iota(jnp.int32, (SEG, GROUP * SEG), 1), SEG
        )
        key_doc = jnp.zeros((SEG, GROUP * SEG), jnp.int32)
        query_doc = jnp.zeros((SEG, GROUP * SEG), jnp.int32)
        for end in ends:
            key_doc = key_doc + (key_pos >= end).astype(jnp.int32)
            query_doc = query_doc + (query_pos >= end).astype(jnp.int32)
        allowed = (key_doc == query_doc) & (key_pos <= query_pos)
        rows = slice(base, base + SEG)
        for h in range(KV):
            kv = slice(h * HEAD, (h + 1) * HEAD)
            cols = [
                slice((h * GROUP + g) * HEAD, (h * GROUP + g + 1) * HEAD)
                for g in range(GROUP)
            ]
            q = jnp.concatenate([sq_in[rows, c] for c in cols], axis=0)
            do = jnp.concatenate([sdo_in[rows, c] for c in cols], axis=0)
            k = sk_in[rows, kv]
            v = sv_in[rows, kv]
            s = jnp.where(allowed, nt(k, q), NEG)
            e = jnp.exp2((s - jnp.max(s, axis=0, keepdims=True)) * SCALE2)
            p = e * (1.0 / jnp.sum(e, axis=0, keepdims=True))
            gp = nt(v, do)
            delta = jnp.sum(p * gp, axis=0, keepdims=True)
            gs = (p * (gp - delta)).astype(jnp.bfloat16)
            sdv_o[rows, kv] = nn(p.astype(jnp.bfloat16), do).astype(jnp.bfloat16)
            sdk_o[rows, kv] = (nn(gs, q) * SCALE).astype(jnp.bfloat16)
            dq = (tn(gs, k) * SCALE).astype(jnp.bfloat16)
            for g, c in enumerate(cols):
                sdq_o[rows, c] = dq[g * SEG : (g + 1) * SEG]

    for i in (6, 7, 0, 1):
        loads[i].wait()
    for h in range(KV):
        for g in range(GROUP):
            c = slice((h * GROUP + g) * HEAD, (h * GROUP + g + 1) * HEAD)
            q_s[h, g * LONG : (g + 1) * LONG] = q_in[:, c]
            do_s[h, g * LONG : (g + 1) * LONG] = do_in[:, c]

    def keys_of(ref, c, h):
        part = ref[pl.ds(c * PER, PER), :, h * HEAD : (h + 1) * HEAD]
        return part.reshape(CHUNK, HEAD)

    def scores(c, causal):
        for h in range(KV):
            s = nt(keys_of(k_all, c, h), q_s[h])
            if causal is not None:
                s = jnp.where(causal, s, NEG)
            m = jnp.max(s, axis=0, keepdims=True)
            e = jnp.exp2((s - m) * SCALE2)
            e_s[h, c] = e
            m_s[h, c] = m
            l_s[h, c] = jnp.sum(e, axis=0, keepdims=True)

    def score_step(c, _):
        for b in range(PER):
            k_copy(me, c * PER + b).wait_recv()
        scores(c, None)
        return 0

    lax.fori_loop(0, row, score_step, 0)

    def wait_k(b, _):
        k_copy(me, row * PER + b).wait_recv()
        return 0

    lax.fori_loop(0, col, wait_k, 0)
    key_pos = lax.broadcasted_iota(jnp.int32, (CHUNK, ROWS), 0)
    query_pos = lax.rem(lax.broadcasted_iota(jnp.int32, (CHUNK, ROWS), 1), LONG)
    scores(row, key_pos <= query_pos + col * LONG)

    for h in range(KV):
        top = lax.fori_loop(
            0, row, lambda c, t: jnp.maximum(t, m_s[h, c]), m_s[h, row]
        )
        sums = lax.fori_loop(
            0,
            row + 1,
            lambda c, t: t + l_s[h, c] * jnp.exp2((m_s[h, c] - top) * SCALE2),
            jnp.zeros((1, ROWS), jnp.float32),
        )
        inverse = 1.0 / sums

        def weigh(c, _):
            m_s[h, c] = jnp.exp2((m_s[h, c] - top) * SCALE2) * inverse
            return 0

        lax.fori_loop(0, row + 1, weigh, 0)

    def value_grads(c):
        for h in range(KV):
            p = e_s[h, c] * m_s[h, c]
            e_s[h, c] = p
            dv = nn(p.astype(jnp.bfloat16), do_s[h])
            dv_out[pl.ds(c * PER, PER), :, h * HEAD : (h + 1) * HEAD] = dv.astype(
                jnp.bfloat16
            ).reshape(PER, LONG, HEAD)

    def value_step(c, _):
        value_grads(c)
        for b in range(PER):
            dv_copy(c * PER + b, me).start()
        return 0

    lax.fori_loop(0, row, value_step, 0)
    value_grads(row)

    def send_dv(b, _):
        dv_copy(row * PER + b, me).start()
        return 0

    lax.fori_loop(0, col, send_dv, 0)

    def prob_grads(c):
        for h in range(KV):
            gp = nt(keys_of(v_all, c, h), do_s[h])
            gp_s[h, c] = gp
            d_s[h] += jnp.sum(e_s[h, c] * gp, axis=0, keepdims=True)

    d_s[...] = jnp.zeros_like(d_s)

    def prob_step(c, _):
        for b in range(PER):
            v_copy(me, c * PER + b).wait_recv()
        prob_grads(c)
        return 0

    lax.fori_loop(0, row, prob_step, 0)

    def wait_v(b, _):
        v_copy(me, row * PER + b).wait_recv()
        return 0

    lax.fori_loop(0, col, wait_v, 0)
    prob_grads(row)

    def key_grads(c):
        for h in range(KV):
            gs = (e_s[h, c] * (gp_s[h, c] - d_s[h])).astype(jnp.bfloat16)
            gs_s[h, c] = gs
            dk = nn(gs, q_s[h]) * SCALE
            dk_out[pl.ds(c * PER, PER), :, h * HEAD : (h + 1) * HEAD] = dk.astype(
                jnp.bfloat16
            ).reshape(PER, LONG, HEAD)

    def key_step(c, _):
        key_grads(c)
        for b in range(PER):
            dk_copy(c * PER + b, me).start()
        return 0

    lax.fori_loop(0, row, key_step, 0)
    key_grads(row)

    def send_dk(b, _):
        dk_copy(row * PER + b, me).start()
        return 0

    lax.fori_loop(0, col, send_dk, 0)

    for h in range(KV):
        dq = lax.fori_loop(
            0,
            row + 1,
            lambda c, t: t + tn(gs_s[h, c], keys_of(k_all, c, h)),
            jnp.zeros((ROWS, HEAD), jnp.float32),
        )
        dq = (dq * SCALE).astype(jnp.bfloat16)
        for g in range(GROUP):
            c = slice((h * GROUP + g) * HEAD, (h * GROUP + g + 1) * HEAD)
            dq_o[:, c] = dq[g * LONG : (g + 1) * LONG]

    def add_dv(i, t):
        j = N - 1 - i
        dv_copy(me, j).wait_recv()
        return t + dv_in[j].astype(jnp.float32)

    def add_dk(i, t):
        j = N - 1 - i
        dk_copy(me, j).wait_recv()
        return t + dk_in[j].astype(jnp.float32)

    dv = lax.fori_loop(0, N - 1 - me, add_dv, dv_out[me].astype(jnp.float32))
    dv_o[...] = dv.astype(jnp.bfloat16)
    dk = lax.fori_loop(0, N - 1 - me, add_dk, dk_out[me].astype(jnp.float32))
    dk_o[...] = dk.astype(jnp.bfloat16)

    def sent_kv(i, _):
        k_copy(N - 1 - i, me).wait_send()
        v_copy(N - 1 - i, me).wait_send()
        return 0

    def sent_grads(j, _):
        dv_copy(j, me).wait_send()
        dk_copy(j, me).wait_send()
        return 0

    lax.fori_loop(0, N - 1 - me, sent_kv, 0)
    lax.fori_loop(0, me, sent_grads, 0)


def write_results(*refs):
    sem = refs[12]
    copies = [pltpu.make_async_copy(refs[i], refs[6 + i], sem.at[i]) for i in range(6)]
    for copy in copies:
        copy.start()
    for copy in copies:
        copy.wait()


def on_device(lq, lk, lv, ldo, sq, sk, sv, sdo, lens):
    bf, f32 = jnp.bfloat16, jnp.float32
    args = (lq[0], lk[0], lv[0], ldo[0], sq[0], sk[0], sv[0], sdo[0], lens)
    kv, qw = KV * HEAD, KV * GROUP * HEAD
    shapes = [(LONG, qw), (LONG, kv), (LONG, kv), (SHORT, qw), (SHORT, kv), (SHORT, kv)]
    any_spec = pl.BlockSpec(memory_space=pltpu.HBM)
    vmem_spec = pl.BlockSpec(memory_space=pltpu.VMEM)
    outs = pl.pallas_call(
        kernel,
        out_shape=[pltpu.VMEM(s, bf) for s in shapes],
        in_specs=[any_spec] * 9,
        out_specs=[vmem_spec] * 6,
        scratch_shapes=[
            pltpu.VMEM((LONG, qw), bf),
            pltpu.VMEM((LONG, qw), bf),
            pltpu.VMEM((SHORT, qw), bf),
            pltpu.VMEM((SHORT, kv), bf),
            pltpu.VMEM((SHORT, kv), bf),
            pltpu.VMEM((SHORT, qw), bf),
            pltpu.VMEM((KV, ROWS, HEAD), bf),
            pltpu.VMEM((KV, ROWS, HEAD), bf),
            pltpu.VMEM((N, LONG, kv), bf),
            pltpu.VMEM((N, LONG, kv), bf),
            pltpu.VMEM((KV, PER, CHUNK, ROWS), f32),
            pltpu.VMEM((KV, PER, CHUNK, ROWS), f32),
            pltpu.VMEM((KV, PER, CHUNK, ROWS), bf),
            pltpu.VMEM((KV, PER, 1, ROWS), f32),
            pltpu.VMEM((KV, PER, 1, ROWS), f32),
            pltpu.VMEM((KV, 1, ROWS), f32),
            pltpu.VMEM((N, LONG, kv), bf),
            pltpu.VMEM((N, LONG, kv), bf),
            pltpu.VMEM((N, LONG, kv), bf),
            pltpu.VMEM((N, LONG, kv), bf),
        ]
        + [pltpu.SMEM((1, 1, DOCS), jnp.int32)]
        + [pltpu.SemaphoreType.DMA((9,))]
        + [pltpu.SemaphoreType.DMA((N,))] * 8,
        compiler_params=pltpu.CompilerParams(
            collective_id=0, has_side_effects=True, vmem_limit_bytes=40 << 20
        ),
        name="attention_grads",
    )(*(pltpu.with_memory_space_constraint(a, pltpu.HBM) for a in args))
    outs = pl.pallas_call(
        write_results,
        out_shape=[jax.ShapeDtypeStruct(s, bf) for s in shapes],
        in_specs=[vmem_spec] * 6,
        out_specs=[any_spec] * 6,
        scratch_shapes=[pltpu.SemaphoreType.DMA((6,))],
        compiler_params=pltpu.CompilerParams(vmem_limit_bytes=1 << 20),
        name="write_results",
    )(*(pltpu.with_memory_space_constraint(o, pltpu.VMEM) for o in outs))
    return tuple(o[None] for o in outs)


def solution(mesh):
    spec = P("dp", "context", "head")
    return jax.shard_map(
        on_device,
        mesh=mesh,
        in_specs=(spec,) * 8 + (P("dp", "context", None),),
        out_specs=(spec,) * 6,
        check_vma=False,
    )
```

```python
import math

import jax
import jax.numpy as jnp
from jax import lax
from jax.experimental import pallas as pl
from jax.experimental.pallas import tpu as pltpu
from jax.sharding import PartitionSpec as P

HEAD = 128
KV = 2
GROUP = 8
LONG = 64
SHORT = 128
SEG = 32
DOCS = 7
N = 16
PER = 4
CHUNK = PER * LONG
ROWS = GROUP * LONG
QW = GROUP * HEAD
MESH = pl.DeviceIdType.MESH
SCALE = 1.0 / math.sqrt(HEAD)
SCALE2 = SCALE * math.log2(math.e)
NEG = -1e30
NT = (((1,), (1,)), ((), ()))
TN = (((0,), (0,)), ((), ()))


def nt(a, b):
    return lax.dot_general(a, b, NT, preferred_element_type=jnp.float32)


def tn(a, b):
    return lax.dot_general(a, b, TN, preferred_element_type=jnp.float32)


def nn(a, b):
    return jnp.dot(a, b, preferred_element_type=jnp.float32)


def kernel(
    lq,
    lk,
    lv,
    ldo,
    sq,
    sk,
    sv,
    sdo,
    lens_hbm,
    dq_o,
    dk_o,
    dv_o,
    sdq_o,
    sdk_o,
    sdv_o,
    sq_in,
    sk_in,
    sv_in,
    sdo_in,
    q_in,
    do_in,
    q_s,
    do_s,
    k_all,
    v_all,
    e_s,
    gp_s,
    gs_s,
    m_s,
    l_s,
    acc_s,
    dv_out,
    dk_out,
    dv_in,
    dk_in,
    dq_out,
    dq_in,
    lens,
    in_sem,
    k_send_x,
    k_send_z,
    k_recv,
    v_send_x,
    v_send_z,
    v_recv,
    dv_send,
    dv_recv,
    dk_send,
    dk_recv,
    q_sem,
    do_sem,
    dq_sem,
):
    me = lax.axis_index("context")
    dp = lax.axis_index("dp")
    hd = lax.axis_index("head")
    x = me // PER
    z = me % PER
    mine = (x >= 2).astype(jnp.int32)
    other = 1 - mine
    low = jnp.minimum(x, PER - 1 - x)
    high = PER - 1 - low
    is_outer = high == PER - 1
    partner = (PER - 1 - x) * PER + z
    kv_mine = pl.ds(pl.multiple_of(mine * HEAD, HEAD), HEAD)
    q_mine = pl.ds(pl.multiple_of(mine * QW, QW), QW)
    q_other = pl.ds(pl.multiple_of(other * QW, QW), QW)

    def dev(j):
        return (dp, j, hd)

    barrier = pltpu.get_barrier_semaphore()
    for d in range(1, N):
        pl.semaphore_signal(
            barrier, inc=1, device_id=dev(lax.rem(me + d, N)), device_id_type=MESH
        )

    loads = [
        pltpu.make_async_copy(src, dst, in_sem.at[i])
        for i, (src, dst) in enumerate(
            (
                (lk.at[:, kv_mine], k_all.at[me]),
                (lv.at[:, kv_mine], v_all.at[me]),
                (sq, sq_in),
                (sk, sk_in),
                (sdo, sdo_in),
                (sv, sv_in),
                (lens_hbm, lens),
                (lq.at[:, q_mine], q_in.at[mine]),
                (ldo.at[:, q_mine], do_in.at[mine]),
            )
        )
    ]
    for load in loads:
        load.start()
    for b in range(PER):

        @pl.when(b > z)
        def _():
            k_all[high * PER + b] = jnp.zeros((LONG, HEAD), jnp.bfloat16)
            v_all[high * PER + b] = jnp.zeros((LONG, HEAD), jnp.bfloat16)

    pl.semaphore_wait(barrier, N - 1)

    def copy(src, dst, send, recv, j):
        return pltpu.make_async_remote_copy(src, dst, send, recv, dev(j), MESH)

    def along_x(src, dst, send, recv):
        for r in range(PER):
            h = slice((r // 2) * HEAD, (r // 2 + 1) * HEAD)
            yield (
                (x != r) & (x <= max(r, PER - 1 - r)),
                copy(src.at[:, h], dst.at[me], send.at[r], recv.at[me], r * PER + z),
            )

    def along_z(src, dst, send, recv, b):
        for d in range(PER):
            yield (
                (z != d) & ((b < high) | ((b == high) & (d > z))),
                copy(
                    src,
                    dst.at[b * PER + z],
                    send.at[b * PER + d],
                    recv.at[b * PER + z],
                    x * PER + d,
                ),
            )

    def each(copies, act):
        for on, c in copies:

            @pl.when(on)
            def _():
                act(c)

    def start(c):
        c.start()

    def forward(dst, send_z, recv):
        for b in range(PER):

            @pl.when((x != b) & (b <= high))
            def _():
                copy(
                    dst.at[me], dst.at[b * PER + z], send_z.at[0], recv.at[b * PER + z], me
                ).wait_recv()
                each(along_z(dst.at[b * PER + z], dst, send_z, recv, b), start)

    def wait_row(dst, recv, b):
        for d in range(PER):

            @pl.when((z != d) & ((b < high) | ((b == high) & (d < z))))
            def _():
                copy(
                    dst.at[me], dst.at[b * PER + d], recv.at[b * PER + d], recv.at[b * PER + d], me
                ).wait_recv()

    def q_copy(src, dst, sem):
        return copy(src.at[:, q_other], dst.at[mine], sem.at[0], sem.at[1], partner)

    each(along_x(lk, k_all, k_send_x, k_recv), start)
    each(along_z(lk.at[:, kv_mine], k_all, k_send_z, k_recv, x), start)
    each(along_x(lv, v_all, v_send_x, v_recv), start)
    each(along_z(lv.at[:, kv_mine], v_all, v_send_z, v_recv, x), start)
    q_copy(lq, q_in, q_sem).start()
    q_copy(ldo, do_in, do_sem).start()

    for i in (2, 3, 4, 5, 6):
        loads[i].wait()
    ends = []
    total = jnp.int32(0)
    for i in range(DOCS):
        total = total + lens[0, 0, i]
        ends.append(total)
    outs = []
    for seg in range(SHORT // SEG):
        base = seg * SEG
        key_pos = base + lax.broadcasted_iota(jnp.int32, (SEG, GROUP * SEG), 0)
        query_pos = base + lax.rem(
            lax.broadcasted_iota(jnp.int32, (SEG, GROUP * SEG), 1), SEG
        )
        key_doc = jnp.zeros((SEG, GROUP * SEG), jnp.int32)
        query_doc = jnp.zeros((SEG, GROUP * SEG), jnp.int32)
        for end in ends:
            key_doc = key_doc + (key_pos >= end).astype(jnp.int32)
            query_doc = query_doc + (query_pos >= end).astype(jnp.int32)
        allowed = (key_doc == query_doc) & (key_pos <= query_pos)
        rows = slice(base, base + SEG)
        for h in range(KV):
            kv = slice(h * HEAD, (h + 1) * HEAD)
            cols = [
                slice((h * GROUP + g) * HEAD, (h * GROUP + g + 1) * HEAD)
                for g in range(GROUP)
            ]
            q = jnp.concatenate([sq_in[rows, c] for c in cols], axis=0)
            do = jnp.concatenate([sdo_in[rows, c] for c in cols], axis=0)
            k = sk_in[rows, kv]
            v = sv_in[rows, kv]
            s = jnp.where(allowed, nt(k, q), NEG)
            e = jnp.exp2((s - jnp.max(s, axis=0, keepdims=True)) * SCALE2)
            p = e * (1.0 / jnp.sum(e, axis=0, keepdims=True))
            gp = nt(v, do)
            delta = jnp.sum(p * gp, axis=0, keepdims=True)
            gs = (p * (gp - delta)).astype(jnp.bfloat16)
            sdv_o[rows, kv] = nn(p.astype(jnp.bfloat16), do).astype(jnp.bfloat16)
            sdk_o[rows, kv] = (nn(gs, q) * SCALE).astype(jnp.bfloat16)
            dq = (tn(gs, k) * SCALE).astype(jnp.bfloat16)
            for g, c in enumerate(cols):
                sdq_o[rows, c] = dq[g * SEG : (g + 1) * SEG]

    for i in (0, 1):
        loads[i].wait()
    forward(k_all, k_send_z, k_recv)
    forward(v_all, v_send_z, v_recv)

    def spread(src, dst, p):
        for g in range(GROUP):
            dst[p, g * LONG : (g + 1) * LONG] = src[p, :, g * HEAD : (g + 1) * HEAD]

    loads[7].wait()
    spread(q_in, q_s, mine)
    q_copy(lq, q_in, q_sem).wait_recv()
    spread(q_in, q_s, other)

    three = jnp.int32(3)
    items = [
        (0, 1, jnp.int32(0)),
        (1, 1, jnp.int32(1)),
        (2, 1, jnp.int32(2)),
        (3, is_outer.astype(jnp.int32), jnp.where(is_outer, three, 0)),
        (4, 0, jnp.where(is_outer, 0, jnp.int32(1))),
    ]
    offset = lax.broadcasted_iota(jnp.int32, (CHUNK, ROWS), 0) - lax.rem(
        lax.broadcasted_iota(jnp.int32, (CHUNK, ROWS), 1), LONG
    )

    def keys_of(ref, c):
        return ref[pl.ds(c * PER, PER)].reshape(CHUNK, HEAD)

    def scores(item):
        i, p, c = item
        own = jnp.where(p == 1, high, low)
        s = nt(keys_of(k_all, c), q_s[p])
        s = jnp.where(offset <= (own - c) * CHUNK + z * LONG, s, NEG)
        m = jnp.max(s, axis=0, keepdims=True)
        e = jnp.exp2((s - m) * SCALE2)
        e_s[i] = e
        m_s[i] = m
        l_s[i] = jnp.sum(e, axis=0, keepdims=True)

    for b in range(PER):
        wait_row(k_all, k_recv, b)
    for item in items:
        scores(item)

    def tops(values, low_value, combine):
        third = values[3]
        high_part = combine(combine(values[0], values[1]), values[2])
        high_part = combine(high_part, jnp.where(is_outer, third, low_value))
        low_part = combine(values[4], jnp.where(is_outer, low_value, third))
        return high_part, low_part

    def per_item(pair):
        return [pair[0]] * 3 + [jnp.where(is_outer, pair[0], pair[1]), pair[1]]

    m = [m_s[i] for i in range(5)]
    top = per_item(tops(m, NEG, jnp.maximum))
    factor = [jnp.exp2((m[i] - top[i]) * SCALE2) for i in range(5)]
    total = per_item(tops([factor[i] * l_s[i] for i in range(5)], 0.0, jnp.add))
    weight = [factor[i] / total[i] for i in range(5)]

    loads[8].wait()
    spread(do_in, do_s, mine)
    q_copy(ldo, do_in, do_sem).wait_recv()
    spread(do_in, do_s, other)

    def grad_copy(src, dst, send, recv, b, d):
        j = b * PER + d
        return copy(src.at[j], dst.at[me], send.at[j], recv.at[me], j)

    def is_sent(b, d):
        return (me != b * PER + d) & ((b < high) | ((b == high) & (d <= z)))

    def send_chunk(src, dst, send, recv, b):
        part = acc_s[b].astype(jnp.bfloat16).reshape(PER, LONG, HEAD)
        src[b * PER : (b + 1) * PER] = part
        for d in range(PER):

            @pl.when(is_sent(b, d))
            def _():
                grad_copy(src, dst, send, recv, b, d).start()

    def shares(product, src, dst, send, recv):
        acc_s[...] = jnp.zeros_like(acc_s)
        for k in (4, 3, 0, 1, 2):
            i, p, c = items[k]
            acc_s[c] += product(i, p)
            if k < 3:
                send_chunk(src, dst, send, recv, k)
            if k == 3:

                @pl.when(is_outer)
                def _():
                    send_chunk(src, dst, send, recv, 3)

    def value_product(i, p):
        e = e_s[i] * weight[i]
        e_s[i] = e
        return nn(e.astype(jnp.bfloat16), do_s[p])

    shares(value_product, dv_out, dv_in, dv_send, dv_recv)

    for b in range(PER):
        wait_row(v_all, v_recv, b)
    delta = []
    for i, p, c in items:
        gp = nt(keys_of(v_all, c), do_s[p])
        gp_s[i] = gp
        delta.append(jnp.sum(e_s[i] * gp, axis=0, keepdims=True))
    delta = per_item(tops(delta, 0.0, jnp.add))

    def key_product(i, p):
        gs = (e_s[i] * (gp_s[i] - delta[i])).astype(jnp.bfloat16)
        gs_s[i] = gs
        return nn(gs, q_s[p]) * SCALE

    shares(key_product, dk_out, dk_in, dk_send, dk_recv)

    def query_grads():
        first = tn(gs_s[4], keys_of(k_all, items[4][2]))
        third = tn(gs_s[3], keys_of(k_all, items[3][2]))
        low_grad = first + jnp.where(is_outer, 0.0, third)
        high_grad = jnp.where(is_outer, third, 0.0)
        for k in range(3):
            high_grad = high_grad + tn(gs_s[k], keys_of(k_all, items[k][2]))
        return low_grad, high_grad

    low_grad, high_grad = query_grads()
    low_grad = (low_grad * SCALE).astype(jnp.bfloat16)
    high_grad = (high_grad * SCALE).astype(jnp.bfloat16)
    is_high = mine == 1
    theirs = jnp.where(is_high, low_grad, high_grad)
    ours = jnp.where(is_high, high_grad, low_grad)
    for g in range(GROUP):
        dq_out[:, g * HEAD : (g + 1) * HEAD] = theirs[g * LONG : (g + 1) * LONG]
    dq_copy = copy(dq_out, dq_in, dq_sem.at[0], dq_sem.at[1], partner)
    dq_copy.start()
    for g in range(GROUP):
        for h in range(KV):

            @pl.when(mine == h)
            def _():
                c = slice((h * GROUP + g) * HEAD, (h * GROUP + g + 1) * HEAD)
                dq_o[:, c] = ours[g * LONG : (g + 1) * LONG]

    def sums(src, dst, recv, out):
        for h in range(KV):
            kv = slice(h * HEAD, (h + 1) * HEAD)

            @pl.when(mine == h)
            def _():
                acc_s[0, :LONG] = src[me].astype(jnp.float32)

            @pl.when(mine != h)
            def _():
                acc_s[0, :LONG] = jnp.zeros((LONG, HEAD), jnp.float32)

            for r in (2 * h, 2 * h + 1):
                last = max(r, PER - 1 - r)
                for d in range(PER):
                    j = r * PER + d

                    @pl.when((me != j) & ((x < last) | ((x == last) & (z <= d))))
                    def _():
                        copy(src.at[me], dst.at[j], recv.at[j], recv.at[j], me).wait_recv()
                        acc_s[0, :LONG] += dst[j].astype(jnp.float32)

            out[:, kv] = acc_s[0, :LONG].astype(jnp.bfloat16)

    sums(dv_out, dv_in, dv_recv, dv_o)
    sums(dk_out, dk_in, dk_recv, dk_o)
    dq_copy.wait_recv()
    for h in range(KV):

        @pl.when(mine != h)
        def _():
            dq_o[:, h * QW : (h + 1) * QW] = dq_in[...]

    def wait_send(c):
        c.wait_send()

    each(along_x(lk, k_all, k_send_x, k_recv), wait_send)
    each(along_x(lv, v_all, v_send_x, v_recv), wait_send)
    for b in range(PER):
        each(along_z(k_all.at[b * PER + z], k_all, k_send_z, k_recv, b), wait_send)
        each(along_z(v_all.at[b * PER + z], v_all, v_send_z, v_recv, b), wait_send)
        for d in range(PER):

            @pl.when(is_sent(b, d))
            def _():
                grad_copy(dv_out, dv_in, dv_send, dv_recv, b, d).wait_send()
                grad_copy(dk_out, dk_in, dk_send, dk_recv, b, d).wait_send()

    q_copy(lq, q_in, q_sem).wait_send()
    q_copy(ldo, do_in, do_sem).wait_send()
    dq_copy.wait_send()


def write_results(*refs):
    sem = refs[12]
    copies = [pltpu.make_async_copy(refs[i], refs[6 + i], sem.at[i]) for i in range(6)]
    for copy in copies:
        copy.start()
    for copy in copies:
        copy.wait()


def on_device(lq, lk, lv, ldo, sq, sk, sv, sdo, lens):
    bf, f32 = jnp.bfloat16, jnp.float32
    args = (lq[0], lk[0], lv[0], ldo[0], sq[0], sk[0], sv[0], sdo[0], lens)
    kv, qw = KV * HEAD, KV * GROUP * HEAD
    shapes = [(LONG, qw), (LONG, kv), (LONG, kv), (SHORT, qw), (SHORT, kv), (SHORT, kv)]
    any_spec = pl.BlockSpec(memory_space=pltpu.HBM)
    vmem_spec = pl.BlockSpec(memory_space=pltpu.VMEM)
    outs = pl.pallas_call(
        kernel,
        out_shape=[pltpu.VMEM(s, bf) for s in shapes],
        in_specs=[any_spec] * 9,
        out_specs=[vmem_spec] * 6,
        scratch_shapes=[
            pltpu.VMEM((SHORT, qw), bf),
            pltpu.VMEM((SHORT, kv), bf),
            pltpu.VMEM((SHORT, kv), bf),
            pltpu.VMEM((SHORT, qw), bf),
            pltpu.VMEM((KV, LONG, QW), bf),
            pltpu.VMEM((KV, LONG, QW), bf),
            pltpu.VMEM((KV, ROWS, HEAD), bf),
            pltpu.VMEM((KV, ROWS, HEAD), bf),
            pltpu.VMEM((N, LONG, HEAD), bf),
            pltpu.VMEM((N, LONG, HEAD), bf),
            pltpu.VMEM((5, CHUNK, ROWS), f32),
            pltpu.VMEM((5, CHUNK, ROWS), f32),
            pltpu.VMEM((5, CHUNK, ROWS), bf),
            pltpu.VMEM((5, 1, ROWS), f32),
            pltpu.VMEM((5, 1, ROWS), f32),
            pltpu.VMEM((PER, CHUNK, HEAD), f32),
            pltpu.VMEM((N, LONG, HEAD), bf),
            pltpu.VMEM((N, LONG, HEAD), bf),
            pltpu.VMEM((N, LONG, HEAD), bf),
            pltpu.VMEM((N, LONG, HEAD), bf),
            pltpu.VMEM((LONG, QW), bf),
            pltpu.VMEM((LONG, QW), bf),
            pltpu.SMEM((1, 1, DOCS), jnp.int32),
            pltpu.SemaphoreType.DMA((9,)),
        ]
        + [pltpu.SemaphoreType.DMA((n,)) for n in (PER, N, N) * 2 + (N,) * 4 + (2,) * 3],
        compiler_params=pltpu.CompilerParams(
            collective_id=0, has_side_effects=True, vmem_limit_bytes=40 << 20
        ),
        name="attention_grads",
    )(*(pltpu.with_memory_space_constraint(a, pltpu.HBM) for a in args))
    outs = pl.pallas_call(
        write_results,
        out_shape=[jax.ShapeDtypeStruct(s, bf) for s in shapes],
        in_specs=[vmem_spec] * 6,
        out_specs=[any_spec] * 6,
        scratch_shapes=[pltpu.SemaphoreType.DMA((6,))],
        compiler_params=pltpu.CompilerParams(vmem_limit_bytes=1 << 20),
        name="write_results",
    )(*(pltpu.with_memory_space_constraint(o, pltpu.VMEM) for o in outs))
    return tuple(o[None] for o in outs)


def solution(mesh):
    spec = P("dp", "context", "head")
    return jax.shard_map(
        on_device,
        mesh=mesh,
        in_specs=(spec,) * 8 + (P("dp", "context", None),),
        out_specs=(spec,) * 6,
        check_vma=False,
    )
```

```python
import math

import jax
import jax.numpy as jnp
from jax import lax
from jax.experimental import pallas as pl
from jax.experimental.pallas import tpu as pltpu
from jax.sharding import PartitionSpec as P

HEAD = 128
KV = 2
GROUP = 8
LONG = 64
SHORT = 128
SEG = 32
DOCS = 7
N = 16
PER = 4
CHUNK = PER * LONG
ROWS = GROUP * LONG
QW = GROUP * HEAD
MESH = pl.DeviceIdType.MESH
SCALE = 1.0 / math.sqrt(HEAD)
SCALE2 = SCALE * math.log2(math.e)
NEG = -1e30
NT = (((1,), (1,)), ((), ()))
TN = (((0,), (0,)), ((), ()))


def nt(a, b):
    return lax.dot_general(a, b, NT, preferred_element_type=jnp.float32)


def tn(a, b):
    return lax.dot_general(a, b, TN, preferred_element_type=jnp.float32)


def nn(a, b):
    return jnp.dot(a, b, preferred_element_type=jnp.float32)


def kernel(
    lq,
    lk,
    lv,
    ldo,
    sq,
    sk,
    sv,
    sdo,
    lens_hbm,
    dq_o,
    dk_o,
    dv_o,
    sdq_o,
    sdk_o,
    sdv_o,
    sq_in,
    sk_in,
    sv_in,
    sdo_in,
    q_in,
    do_in,
    q_s,
    do_s,
    k_all,
    v_all,
    e_s,
    gp_s,
    gs_s,
    w_s,
    d_s,
    acc_s,
    dv_out,
    dk_out,
    dv_in,
    dk_in,
    dq_out,
    dq_in,
    lens,
    in_sem,
    k_send_x,
    k_send_z,
    k_recv,
    v_send_x,
    v_send_z,
    v_recv,
    dv_send,
    dv_recv,
    dk_send,
    dk_recv,
    q_sem,
    do_sem,
    dq_sem,
):
    me = lax.axis_index("context")
    dp = lax.axis_index("dp")
    hd = lax.axis_index("head")
    x = me // PER
    z = me % PER
    crossed = hd == 0

    def partner_of(r):
        return jnp.where(crossed, PER - 1 - r, r + 1 - 2 * (r % 2))

    def head_of(r):
        return (r > partner_of(r)).astype(jnp.int32)

    def last_of(r):
        return jnp.maximum(r, partner_of(r))

    mine = head_of(x)
    other = 1 - mine
    high = last_of(x)
    partner = partner_of(x) * PER + z
    kv_mine = pl.ds(pl.multiple_of(mine * HEAD, HEAD), HEAD)
    q_mine = pl.ds(pl.multiple_of(mine * QW, QW), QW)
    q_other = pl.ds(pl.multiple_of(other * QW, QW), QW)

    def dev(j):
        return (dp, j, hd)

    barrier = pltpu.get_barrier_semaphore()
    for d in range(1, N):
        pl.semaphore_signal(
            barrier, inc=1, device_id=dev(lax.rem(me + d, N)), device_id_type=MESH
        )

    loads = [
        pltpu.make_async_copy(src, dst, in_sem.at[i])
        for i, (src, dst) in enumerate(
            (
                (lk.at[:, kv_mine], k_all.at[me]),
                (lv.at[:, kv_mine], v_all.at[me]),
                (sq, sq_in),
                (sk, sk_in),
                (sdo, sdo_in),
                (sv, sv_in),
                (lens_hbm, lens),
                (lq.at[:, q_mine], q_in.at[mine]),
                (ldo.at[:, q_mine], do_in.at[mine]),
            )
        )
    ]
    for load in loads:
        load.start()
    for b in range(PER):

        @pl.when(b > z)
        def _():
            k_all[high * PER + b] = jnp.zeros((LONG, HEAD), jnp.bfloat16)
            v_all[high * PER + b] = jnp.zeros((LONG, HEAD), jnp.bfloat16)

    pl.semaphore_wait(barrier, N - 1)

    def copy(src, dst, send, recv, j):
        return pltpu.make_async_remote_copy(src, dst, send, recv, dev(j), MESH)

    def along_x(src, dst, send, recv):
        for r in range(PER):
            h = pl.ds(pl.multiple_of(head_of(r) * HEAD, HEAD), HEAD)
            yield (
                (x != r) & (x <= last_of(r)),
                copy(src.at[:, h], dst.at[me], send.at[r], recv.at[me], r * PER + z),
            )

    def along_z(src, dst, send, recv, b):
        for d in range(PER):
            yield (
                (z != d) & ((b < high) | ((b == high) & (d > z))),
                copy(
                    src,
                    dst.at[b * PER + z],
                    send.at[b * PER + d],
                    recv.at[b * PER + z],
                    x * PER + d,
                ),
            )

    def each(copies, act):
        for on, c in copies:

            @pl.when(on)
            def _():
                act(c)

    def start(c):
        c.start()

    def forward(dst, send_z, recv):
        for b in range(PER):

            @pl.when((x != b) & (b <= high))
            def _():
                copy(
                    dst.at[me], dst.at[b * PER + z], send_z.at[0], recv.at[b * PER + z], me
                ).wait_recv()
                each(along_z(dst.at[b * PER + z], dst, send_z, recv, b), start)

    def wait_row(dst, recv, b):
        for d in range(PER):

            @pl.when((z != d) & ((b < high) | ((b == high) & (d < z))))
            def _():
                copy(
                    dst.at[me], dst.at[b * PER + d], recv.at[b * PER + d], recv.at[b * PER + d], me
                ).wait_recv()

    def q_copy(src, dst, sem):
        return copy(src.at[:, q_other], dst.at[mine], sem.at[0], sem.at[1], partner)

    each(along_x(lk, k_all, k_send_x, k_recv), start)
    each(along_z(lk.at[:, kv_mine], k_all, k_send_z, k_recv, x), start)
    each(along_x(lv, v_all, v_send_x, v_recv), start)
    each(along_z(lv.at[:, kv_mine], v_all, v_send_z, v_recv, x), start)
    q_copy(lq, q_in, q_sem).start()
    q_copy(ldo, do_in, do_sem).start()

    for i in (2, 3, 4, 5, 6):
        loads[i].wait()
    ends = []
    total = jnp.int32(0)
    for i in range(DOCS):
        total = total + lens[0, 0, i]
        ends.append(total)
    outs = []
    for seg in range(SHORT // SEG):
        base = seg * SEG
        key_pos = base + lax.broadcasted_iota(jnp.int32, (SEG, GROUP * SEG), 0)
        query_pos = base + lax.rem(
            lax.broadcasted_iota(jnp.int32, (SEG, GROUP * SEG), 1), SEG
        )
        key_doc = jnp.zeros((SEG, GROUP * SEG), jnp.int32)
        query_doc = jnp.zeros((SEG, GROUP * SEG), jnp.int32)
        for end in ends:
            key_doc = key_doc + (key_pos >= end).astype(jnp.int32)
            query_doc = query_doc + (query_pos >= end).astype(jnp.int32)
        allowed = (key_doc == query_doc) & (key_pos <= query_pos)
        rows = slice(base, base + SEG)
        for h in range(KV):
            kv = slice(h * HEAD, (h + 1) * HEAD)
            cols = [
                slice((h * GROUP + g) * HEAD, (h * GROUP + g + 1) * HEAD)
                for g in range(GROUP)
            ]
            q = jnp.concatenate([sq_in[rows, c] for c in cols], axis=0)
            do = jnp.concatenate([sdo_in[rows, c] for c in cols], axis=0)
            k = sk_in[rows, kv]
            v = sv_in[rows, kv]
            s = jnp.where(allowed, nt(k, q), NEG)
            e = jnp.exp2((s - jnp.max(s, axis=0, keepdims=True)) * SCALE2)
            p = e * (1.0 / jnp.sum(e, axis=0, keepdims=True))
            gp = nt(v, do)
            delta = jnp.sum(p * gp, axis=0, keepdims=True)
            gs = (p * (gp - delta)).astype(jnp.bfloat16)
            sdv_o[rows, kv] = nn(p.astype(jnp.bfloat16), do).astype(jnp.bfloat16)
            sdk_o[rows, kv] = (nn(gs, q) * SCALE).astype(jnp.bfloat16)
            dq = (tn(gs, k) * SCALE).astype(jnp.bfloat16)
            for g, c in enumerate(cols):
                sdq_o[rows, c] = dq[g * SEG : (g + 1) * SEG]

    for i in (0, 1):
        loads[i].wait()
    forward(k_all, k_send_z, k_recv)
    forward(v_all, v_send_z, v_recv)

    def spread(src, dst, p):
        for g in range(GROUP):
            dst[p, g * LONG : (g + 1) * LONG] = src[p, :, g * HEAD : (g + 1) * HEAD]

    offset = lax.broadcasted_iota(jnp.int32, (CHUNK, ROWS), 0) - lax.rem(
        lax.broadcasted_iota(jnp.int32, (CHUNK, ROWS), 1), LONG
    )
    parts = ((mine, x), (other, partner_of(x)))

    def by_count(own, act):
        for n in range(1, PER + 1):

            @pl.when(own == n - 1)
            def _():
                act(n)

    def keys_of(ref, c, n=1):
        return ref[c * PER : (c + n) * PER].reshape(n * CHUNK, HEAD)

    def scores(p, n):
        tops = []
        sums = []
        for c in range(n):
            s = nt(keys_of(k_all, c), q_s[p])
            if c == n - 1:
                s = jnp.where(offset <= z * LONG, s, NEG)
            m = jnp.max(s, axis=0, keepdims=True)
            e = jnp.exp2((s - m) * SCALE2)
            e_s[p, c] = e
            tops.append(m)
            sums.append(jnp.sum(e, axis=0, keepdims=True))
        top = tops[0]
        for m in tops[1:]:
            top = jnp.maximum(top, m)
        factors = [jnp.exp2((m - top) * SCALE2) for m in tops]
        total = factors[0] * sums[0]
        for c in range(1, n):
            total = total + factors[c] * sums[c]
        inverse = 1.0 / total
        for c in range(n):
            w_s[p, c] = factors[c] * inverse

    def grad_copy(src, dst, send, recv, b, d):
        j = b * PER + d
        return copy(src.at[j], dst.at[me], send.at[j], recv.at[me], j)

    def is_sent(b, d):
        return (me != b * PER + d) & ((b < high) | ((b == high) & (d <= z)))

    def send_chunk(src, dst, send, recv, b):
        part = acc_s[b].astype(jnp.bfloat16).reshape(PER, LONG, HEAD)
        src[pl.ds(b * PER, PER)] = part
        for d in range(PER):

            @pl.when(is_sent(b, d))
            def _():
                grad_copy(src, dst, send, recv, b, d).start()

    def shares(product, p, n, rest, dst):
        for c in range(n):
            acc_s[c] += product(p, c)

            @pl.when(c > rest)
            def _():
                send_chunk(*dst, c)

    def value_product(p, c):
        return nn((e_s[p, c] * w_s[p, c]).astype(jnp.bfloat16), do_s[p])

    def key_product(p, c):
        gs = (e_s[p, c] * (w_s[p, c] * (gp_s[p, c] - d_s[p]))).astype(jnp.bfloat16)
        gs_s[p, c] = gs
        return nn(gs, q_s[p]) * SCALE

    def prob_grads(p, n):
        delta = jnp.zeros((1, ROWS), jnp.float32)
        for c in range(n):
            gp = nt(keys_of(v_all, c), do_s[p])
            gp_s[p, c] = gp
            delta = delta + w_s[p, c] * jnp.sum(e_s[p, c] * gp, axis=0, keepdims=True)
        d_s[p] = delta

    def query_grads(p, n):
        gs = gs_s[p, :n].reshape(n * CHUNK, ROWS)
        return (tn(gs, keys_of(k_all, 0, n)) * SCALE).astype(jnp.bfloat16)

    dv_ends = (dv_out, dv_in, dv_send, dv_recv)
    dk_ends = (dk_out, dk_in, dk_send, dk_recv)
    (p1, own1), (p2, own2) = parts
    loads[7].wait()
    spread(q_in, q_s, p1)
    for b in range(PER):
        wait_row(k_all, k_recv, b)
    by_count(own1, lambda n: scores(p1, n))
    acc_s[...] = jnp.zeros_like(acc_s)
    loads[8].wait()
    spread(do_in, do_s, p1)
    by_count(own1, lambda n: shares(value_product, p1, n, own2, dv_ends))
    q_copy(lq, q_in, q_sem).wait_recv()
    spread(q_in, q_s, p2)
    by_count(own2, lambda n: scores(p2, n))
    q_copy(ldo, do_in, do_sem).wait_recv()
    spread(do_in, do_s, p2)
    by_count(own2, lambda n: shares(value_product, p2, n, -1, dv_ends))
    for b in range(PER):
        wait_row(v_all, v_recv, b)
    by_count(own1, lambda n: prob_grads(p1, n))
    acc_s[...] = jnp.zeros_like(acc_s)
    by_count(own1, lambda n: shares(key_product, p1, n, own2, dk_ends))
    by_count(own2, lambda n: prob_grads(p2, n))
    by_count(own2, lambda n: shares(key_product, p2, n, -1, dk_ends))

    def theirs(n):
        grad = query_grads(p2, n)
        for g in range(GROUP):
            dq_out[:, g * HEAD : (g + 1) * HEAD] = grad[g * LONG : (g + 1) * LONG]

    by_count(own2, theirs)
    dq_copy = copy(dq_out, dq_in, dq_sem.at[0], dq_sem.at[1], partner)
    dq_copy.start()

    def ours(n):
        grad = query_grads(p1, n)
        for g in range(GROUP):
            q_in[mine, :, g * HEAD : (g + 1) * HEAD] = grad[g * LONG : (g + 1) * LONG]

    by_count(own1, ours)
    for h in range(KV):

        @pl.when(mine == h)
        def _():
            dq_o[:, h * QW : (h + 1) * QW] = q_in[mine]

    def wait_send(c):
        c.wait_send()

    each(along_x(lk, k_all, k_send_x, k_recv), wait_send)
    each(along_x(lv, v_all, v_send_x, v_recv), wait_send)
    for b in range(PER):
        each(along_z(k_all.at[b * PER + z], k_all, k_send_z, k_recv, b), wait_send)
        each(along_z(v_all.at[b * PER + z], v_all, v_send_z, v_recv, b), wait_send)
        for d in range(PER):

            @pl.when(is_sent(b, d))
            def _():
                grad_copy(dv_out, dv_in, dv_send, dv_recv, b, d).wait_send()
                grad_copy(dk_out, dk_in, dk_send, dk_recv, b, d).wait_send()

    q_copy(lq, q_in, q_sem).wait_send()
    q_copy(ldo, do_in, do_sem).wait_send()
    dq_copy.wait_send()

    def sums(src, dst, recv, out):
        for h in range(KV):
            kv = slice(h * HEAD, (h + 1) * HEAD)

            @pl.when(mine == h)
            def _():
                acc_s[0, :LONG] = src[me].astype(jnp.float32)

            @pl.when(mine != h)
            def _():
                acc_s[0, :LONG] = jnp.zeros((LONG, HEAD), jnp.float32)

            for i in range(2):
                r = jnp.where(crossed, 2 * h + i, 2 * i + h)
                last = last_of(r)
                for d in range(PER):
                    j = r * PER + d

                    @pl.when((me != j) & ((x < last) | ((x == last) & (z <= d))))
                    def _():
                        copy(src.at[me], dst.at[j], recv.at[j], recv.at[j], me).wait_recv()
                        acc_s[0, :LONG] += dst[j].astype(jnp.float32)

            out[:, kv] = acc_s[0, :LONG].astype(jnp.bfloat16)

    sums(dv_out, dv_in, dv_recv, dv_o)
    sums(dk_out, dk_in, dk_recv, dk_o)
    dq_copy.wait_recv()
    for h in range(KV):

        @pl.when(mine != h)
        def _():
            dq_o[:, h * QW : (h + 1) * QW] = dq_in[...]


def write_results(*refs):
    sem = refs[12]
    copies = [pltpu.make_async_copy(refs[i], refs[6 + i], sem.at[i]) for i in range(6)]
    for copy in copies:
        copy.start()
    for copy in copies:
        copy.wait()


def on_device(lq, lk, lv, ldo, sq, sk, sv, sdo, lens):
    bf, f32 = jnp.bfloat16, jnp.float32
    args = (lq[0], lk[0], lv[0], ldo[0], sq[0], sk[0], sv[0], sdo[0], lens)
    kv, qw = KV * HEAD, KV * GROUP * HEAD
    shapes = [(LONG, qw), (LONG, kv), (LONG, kv), (SHORT, qw), (SHORT, kv), (SHORT, kv)]
    any_spec = pl.BlockSpec(memory_space=pltpu.HBM)
    vmem_spec = pl.BlockSpec(memory_space=pltpu.VMEM)
    outs = pl.pallas_call(
        kernel,
        out_shape=[pltpu.VMEM(s, bf) for s in shapes],
        in_specs=[any_spec] * 9,
        out_specs=[vmem_spec] * 6,
        scratch_shapes=[
            pltpu.VMEM((SHORT, qw), bf),
            pltpu.VMEM((SHORT, kv), bf),
            pltpu.VMEM((SHORT, kv), bf),
            pltpu.VMEM((SHORT, qw), bf),
            pltpu.VMEM((KV, LONG, QW), bf),
            pltpu.VMEM((KV, LONG, QW), bf),
            pltpu.VMEM((KV, ROWS, HEAD), bf),
            pltpu.VMEM((KV, ROWS, HEAD), bf),
            pltpu.VMEM((N, LONG, HEAD), bf),
            pltpu.VMEM((N, LONG, HEAD), bf),
            pltpu.VMEM((KV, PER, CHUNK, ROWS), f32),
            pltpu.VMEM((KV, PER, CHUNK, ROWS), f32),
            pltpu.VMEM((KV, PER, CHUNK, ROWS), bf),
            pltpu.VMEM((KV, PER, 1, ROWS), f32),
            pltpu.VMEM((KV, 1, ROWS), f32),
            pltpu.VMEM((PER, CHUNK, HEAD), f32),
            pltpu.VMEM((N, LONG, HEAD), bf),
            pltpu.VMEM((N, LONG, HEAD), bf),
            pltpu.VMEM((N, LONG, HEAD), bf),
            pltpu.VMEM((N, LONG, HEAD), bf),
            pltpu.VMEM((LONG, QW), bf),
            pltpu.VMEM((LONG, QW), bf),
            pltpu.SMEM((1, 1, DOCS), jnp.int32),
            pltpu.SemaphoreType.DMA((9,)),
        ]
        + [pltpu.SemaphoreType.DMA((n,)) for n in (PER, N, N) * 2 + (N,) * 4 + (2,) * 3],
        compiler_params=pltpu.CompilerParams(
            collective_id=0, has_side_effects=True, vmem_limit_bytes=40 << 20
        ),
        name="attention_grads",
    )(*(pltpu.with_memory_space_constraint(a, pltpu.HBM) for a in args))
    outs = pl.pallas_call(
        write_results,
        out_shape=[jax.ShapeDtypeStruct(s, bf) for s in shapes],
        in_specs=[vmem_spec] * 6,
        out_specs=[any_spec] * 6,
        scratch_shapes=[pltpu.SemaphoreType.DMA((6,))],
        compiler_params=pltpu.CompilerParams(vmem_limit_bytes=1 << 20),
        name="write_results",
    )(*(pltpu.with_memory_space_constraint(o, pltpu.VMEM) for o in outs))
    return tuple(o[None] for o in outs)


def solution(mesh):
    spec = P("dp", "context", "head")
    return jax.shard_map(
        on_device,
        mesh=mesh,
        in_specs=(spec,) * 8 + (P("dp", "context", None),),
        out_specs=(spec,) * 6,
        check_vma=False,
    )
```

```python
import math

import jax
import jax.numpy as jnp
from jax import lax
from jax.experimental import pallas as pl
from jax.experimental.pallas import tpu as pltpu
from jax.sharding import PartitionSpec as P

HEAD = 128
KV = 2
GROUP = 8
LONG = 64
SHORT = 128
SEG = 32
DOCS = 7
N = 16
PER = 4
CHUNK = PER * LONG
ROWS = GROUP * LONG
QW = GROUP * HEAD
MESH = pl.DeviceIdType.MESH
SCALE = 1.0 / math.sqrt(HEAD)
SCALE2 = SCALE * math.log2(math.e)
NEG = -1e30
NT = (((1,), (1,)), ((), ()))
TN = (((0,), (0,)), ((), ()))


def nt(a, b):
    return lax.dot_general(a, b, NT, preferred_element_type=jnp.float32)


def tn(a, b):
    return lax.dot_general(a, b, TN, preferred_element_type=jnp.float32)


def nn(a, b):
    return jnp.dot(a, b, preferred_element_type=jnp.float32)


def kernel(
    lq,
    lk,
    lv,
    ldo,
    sq,
    sk,
    sv,
    sdo,
    lens_hbm,
    dq_o,
    dk_o,
    dv_o,
    sdq_o,
    sdk_o,
    sdv_o,
    sq_in,
    sk_in,
    sv_in,
    sdo_in,
    q_in,
    do_in,
    q_s,
    do_s,
    k_all,
    v_all,
    e_s,
    gp_s,
    gs_s,
    w_s,
    d_s,
    acc_s,
    dv_out,
    dk_out,
    dv_in,
    dk_in,
    dq_out,
    dq_in,
    lens,
    in_sem,
    k_send_x,
    k_send_z,
    k_recv,
    v_send_x,
    v_send_z,
    v_recv,
    dv_send,
    dv_recv,
    dk_send,
    dk_recv,
    q_sem,
    do_sem,
    dq_sem,
):
    me = lax.axis_index("context")
    dp = lax.axis_index("dp")
    hd = lax.axis_index("head")
    x = me // PER
    z = me % PER
    crossed = hd == 0

    def partner_of(r):
        return jnp.where(crossed, PER - 1 - r, r + 1 - 2 * (r % 2))

    def head_of(r):
        return (r > partner_of(r)).astype(jnp.int32)

    def last_of(r):
        return jnp.maximum(r, partner_of(r))

    mine = head_of(x)
    other = 1 - mine
    high = last_of(x)
    partner = partner_of(x) * PER + z
    kv_mine = pl.ds(pl.multiple_of(mine * HEAD, HEAD), HEAD)
    q_mine = pl.ds(pl.multiple_of(mine * QW, QW), QW)
    q_other = pl.ds(pl.multiple_of(other * QW, QW), QW)

    def dev(j):
        return (dp, j, hd)

    barrier = pltpu.get_barrier_semaphore()
    for d in range(1, N):
        pl.semaphore_signal(
            barrier, inc=1, device_id=dev(lax.rem(me + d, N)), device_id_type=MESH
        )

    loads = [
        pltpu.make_async_copy(src, dst, in_sem.at[i])
        for i, (src, dst) in enumerate(
            (
                (lk.at[:, kv_mine], k_all.at[me]),
                (lv.at[:, kv_mine], v_all.at[me]),
                (sq, sq_in),
                (sk, sk_in),
                (sdo, sdo_in),
                (sv, sv_in),
                (lens_hbm, lens),
                (lq.at[:, q_mine], q_in.at[mine]),
                (ldo.at[:, q_mine], do_in.at[mine]),
            )
        )
    ]
    for load in loads:
        load.start()
    for b in range(PER):

        @pl.when(b > z)
        def _():
            k_all[high * PER + b] = jnp.zeros((LONG, HEAD), jnp.bfloat16)
            v_all[high * PER + b] = jnp.zeros((LONG, HEAD), jnp.bfloat16)

    pl.semaphore_wait(barrier, N - 1)

    def copy(src, dst, send, recv, j):
        return pltpu.make_async_remote_copy(src, dst, send, recv, dev(j), MESH)

    def along_x(src, dst, send, recv):
        for r in range(PER):
            h = pl.ds(pl.multiple_of(head_of(r) * HEAD, HEAD), HEAD)
            yield (
                (x != r) & (x <= last_of(r)),
                copy(src.at[:, h], dst.at[me], send.at[r], recv.at[me], r * PER + z),
            )

    def along_z(src, dst, send, recv, b):
        for d in range(PER):
            yield (
                (z != d) & ((b < high) | ((b == high) & (d > z))),
                copy(
                    src,
                    dst.at[b * PER + z],
                    send.at[b * PER + d],
                    recv.at[b * PER + z],
                    x * PER + d,
                ),
            )

    def to_all(src, dst, send, recv):
        for r in (3, 2, 1, 0):
            h = pl.ds(pl.multiple_of(head_of(r) * HEAD, HEAD), HEAD)
            for d in range(PER):
                j = r * PER + d
                yield (
                    (me != j) & ((x < last_of(r)) | ((x == last_of(r)) & (z <= d))),
                    copy(src.at[:, h], dst.at[me], send.at[j], recv.at[me], j),
                )

    def wait_direct(dst, recv, b):
        for d in range(PER):
            j = b * PER + d

            @pl.when((me != j) & ((b < high) | ((b == high) & (d <= z))))
            def _():
                copy(dst.at[me], dst.at[j], recv.at[j], recv.at[j], me).wait_recv()

    def each(copies, act):
        for on, c in copies:

            @pl.when(on)
            def _():
                act(c)

    def start(c):
        c.start()

    def forward(dst, send_z, recv):
        for b in range(PER):

            @pl.when((x != b) & (b <= high))
            def _():
                copy(
                    dst.at[me], dst.at[b * PER + z], send_z.at[0], recv.at[b * PER + z], me
                ).wait_recv()
                each(along_z(dst.at[b * PER + z], dst, send_z, recv, b), start)

    def wait_row(dst, recv, b):
        for d in range(PER):

            @pl.when((z != d) & ((b < high) | ((b == high) & (d < z))))
            def _():
                copy(
                    dst.at[me], dst.at[b * PER + d], recv.at[b * PER + d], recv.at[b * PER + d], me
                ).wait_recv()

    def q_copy(src, dst, sem):
        return copy(src.at[:, q_other], dst.at[mine], sem.at[0], sem.at[1], partner)

    each(along_x(lv, v_all, v_send_x, v_recv), start)
    each(to_all(lk, k_all, k_send_z, k_recv), start)
    each(along_z(lv.at[:, kv_mine], v_all, v_send_z, v_recv, x), start)
    q_copy(lq, q_in, q_sem).start()
    q_copy(ldo, do_in, do_sem).start()

    for i in (2, 3, 4, 5, 6):
        loads[i].wait()
    ends = []
    total = jnp.int32(0)
    for i in range(DOCS):
        total = total + lens[0, 0, i]
        ends.append(total)
    outs = []
    for seg in range(SHORT // SEG):
        base = seg * SEG
        key_pos = base + lax.broadcasted_iota(jnp.int32, (SEG, GROUP * SEG), 0)
        query_pos = base + lax.rem(
            lax.broadcasted_iota(jnp.int32, (SEG, GROUP * SEG), 1), SEG
        )
        key_doc = jnp.zeros((SEG, GROUP * SEG), jnp.int32)
        query_doc = jnp.zeros((SEG, GROUP * SEG), jnp.int32)
        for end in ends:
            key_doc = key_doc + (key_pos >= end).astype(jnp.int32)
            query_doc = query_doc + (query_pos >= end).astype(jnp.int32)
        allowed = (key_doc == query_doc) & (key_pos <= query_pos)
        rows = slice(base, base + SEG)
        for h in range(KV):
            kv = slice(h * HEAD, (h + 1) * HEAD)
            cols = [
                slice((h * GROUP + g) * HEAD, (h * GROUP + g + 1) * HEAD)
                for g in range(GROUP)
            ]
            q = jnp.concatenate([sq_in[rows, c] for c in cols], axis=0)
            do = jnp.concatenate([sdo_in[rows, c] for c in cols], axis=0)
            k = sk_in[rows, kv]
            v = sv_in[rows, kv]
            s = jnp.where(allowed, nt(k, q), NEG)
            e = jnp.exp2((s - jnp.max(s, axis=0, keepdims=True)) * SCALE2)
            p = e * (1.0 / jnp.sum(e, axis=0, keepdims=True))
            gp = nt(v, do)
            delta = jnp.sum(p * gp, axis=0, keepdims=True)
            gs = (p * (gp - delta)).astype(jnp.bfloat16)
            sdv_o[rows, kv] = nn(p.astype(jnp.bfloat16), do).astype(jnp.bfloat16)
            sdk_o[rows, kv] = (nn(gs, q) * SCALE).astype(jnp.bfloat16)
            dq = (tn(gs, k) * SCALE).astype(jnp.bfloat16)
            for g, c in enumerate(cols):
                sdq_o[rows, c] = dq[g * SEG : (g + 1) * SEG]

    for i in (0, 1):
        loads[i].wait()
    forward(v_all, v_send_z, v_recv)

    def spread(src, dst, p):
        for g in range(GROUP):
            dst[p, g * LONG : (g + 1) * LONG] = src[p, :, g * HEAD : (g + 1) * HEAD]

    offset = lax.broadcasted_iota(jnp.int32, (CHUNK, ROWS), 0) - lax.rem(
        lax.broadcasted_iota(jnp.int32, (CHUNK, ROWS), 1), LONG
    )
    parts = ((mine, x), (other, partner_of(x)))

    def by_count(own, act):
        for n in range(1, PER + 1):

            @pl.when(own == n - 1)
            def _():
                act(n)

    def keys_of(ref, c, n=1):
        return ref[c * PER : (c + n) * PER].reshape(n * CHUNK, HEAD)

    def scores(p, n):
        tops = []
        sums = []
        for c in range(n):
            s = nt(keys_of(k_all, c), q_s[p])
            if c == n - 1:
                s = jnp.where(offset <= z * LONG, s, NEG)
            m = jnp.max(s, axis=0, keepdims=True)
            e = jnp.exp2((s - m) * SCALE2)
            e_s[p, c] = e
            tops.append(m)
            sums.append(jnp.sum(e, axis=0, keepdims=True))
        top = tops[0]
        for m in tops[1:]:
            top = jnp.maximum(top, m)
        factors = [jnp.exp2((m - top) * SCALE2) for m in tops]
        total = factors[0] * sums[0]
        for c in range(1, n):
            total = total + factors[c] * sums[c]
        inverse = 1.0 / total
        for c in range(n):
            w_s[p, c] = factors[c] * inverse

    def grad_copy(src, dst, send, recv, b, d):
        j = b * PER + d
        return copy(src.at[j], dst.at[me], send.at[j], recv.at[me], j)

    def is_sent(b, d):
        return (me != b * PER + d) & ((b < high) | ((b == high) & (d <= z)))

    def send_chunk(src, dst, send, recv, b):
        part = acc_s[b].astype(jnp.bfloat16).reshape(PER, LONG, HEAD)
        src[pl.ds(b * PER, PER)] = part
        for d in range(PER):

            @pl.when(is_sent(b, d))
            def _():
                grad_copy(src, dst, send, recv, b, d).start()

    def shares(product, p, n, rest, dst):
        for c in range(n):
            acc_s[c] += product(p, c)

            @pl.when(c > rest)
            def _():
                send_chunk(*dst, c)

    def value_product(p, c):
        return nn((e_s[p, c] * w_s[p, c]).astype(jnp.bfloat16), do_s[p])

    def key_product(p, c):
        gs = (e_s[p, c] * (w_s[p, c] * (gp_s[p, c] - d_s[p]))).astype(jnp.bfloat16)
        gs_s[p, c] = gs
        return nn(gs, q_s[p]) * SCALE

    def prob_grads(p, n):
        delta = jnp.zeros((1, ROWS), jnp.float32)
        for c in range(n):
            gp = nt(keys_of(v_all, c), do_s[p])
            gp_s[p, c] = gp
            delta = delta + w_s[p, c] * jnp.sum(e_s[p, c] * gp, axis=0, keepdims=True)
        d_s[p] = delta

    def query_grads(p, n):
        gs = gs_s[p, :n].reshape(n * CHUNK, ROWS)
        return (tn(gs, keys_of(k_all, 0, n)) * SCALE).astype(jnp.bfloat16)

    dv_ends = (dv_out, dv_in, dv_send, dv_recv)
    dk_ends = (dk_out, dk_in, dk_send, dk_recv)
    (p1, own1), (p2, own2) = parts
    loads[7].wait()
    spread(q_in, q_s, p1)
    for b in range(PER):
        wait_direct(k_all, k_recv, b)
    by_count(own1, lambda n: scores(p1, n))
    acc_s[...] = jnp.zeros_like(acc_s)
    loads[8].wait()
    spread(do_in, do_s, p1)
    by_count(own1, lambda n: shares(value_product, p1, n, own2, dv_ends))
    q_copy(lq, q_in, q_sem).wait_recv()
    spread(q_in, q_s, p2)
    by_count(own2, lambda n: scores(p2, n))
    q_copy(ldo, do_in, do_sem).wait_recv()
    spread(do_in, do_s, p2)
    by_count(own2, lambda n: shares(value_product, p2, n, -1, dv_ends))
    for b in range(PER):
        wait_row(v_all, v_recv, b)
    by_count(own1, lambda n: prob_grads(p1, n))
    acc_s[...] = jnp.zeros_like(acc_s)
    by_count(own1, lambda n: shares(key_product, p1, n, own2, dk_ends))
    by_count(own2, lambda n: prob_grads(p2, n))
    by_count(own2, lambda n: shares(key_product, p2, n, -1, dk_ends))

    def theirs(n):
        grad = query_grads(p2, n)
        for g in range(GROUP):
            dq_out[:, g * HEAD : (g + 1) * HEAD] = grad[g * LONG : (g + 1) * LONG]

    by_count(own2, theirs)
    dq_copy = copy(dq_out, dq_in, dq_sem.at[0], dq_sem.at[1], partner)
    dq_copy.start()

    def ours(n):
        grad = query_grads(p1, n)
        for g in range(GROUP):
            q_in[mine, :, g * HEAD : (g + 1) * HEAD] = grad[g * LONG : (g + 1) * LONG]

    by_count(own1, ours)
    for h in range(KV):

        @pl.when(mine == h)
        def _():
            dq_o[:, h * QW : (h + 1) * QW] = q_in[mine]

    def wait_send(c):
        c.wait_send()

    each(to_all(lk, k_all, k_send_z, k_recv), wait_send)
    each(along_x(lv, v_all, v_send_x, v_recv), wait_send)
    for b in range(PER):
        each(along_z(v_all.at[b * PER + z], v_all, v_send_z, v_recv, b), wait_send)
        for d in range(PER):

            @pl.when(is_sent(b, d))
            def _():
                grad_copy(dv_out, dv_in, dv_send, dv_recv, b, d).wait_send()
                grad_copy(dk_out, dk_in, dk_send, dk_recv, b, d).wait_send()

    q_copy(lq, q_in, q_sem).wait_send()
    q_copy(ldo, do_in, do_sem).wait_send()
    dq_copy.wait_send()

    def sums(src, dst, recv, out):
        for h in range(KV):
            kv = slice(h * HEAD, (h + 1) * HEAD)

            @pl.when(mine == h)
            def _():
                acc_s[0, :LONG] = src[me].astype(jnp.float32)

            @pl.when(mine != h)
            def _():
                acc_s[0, :LONG] = jnp.zeros((LONG, HEAD), jnp.float32)

            for i in range(2):
                r = jnp.where(crossed, 2 * h + i, 2 * i + h)
                last = last_of(r)
                for d in range(PER):
                    j = r * PER + d

                    @pl.when((me != j) & ((x < last) | ((x == last) & (z <= d))))
                    def _():
                        copy(src.at[me], dst.at[j], recv.at[j], recv.at[j], me).wait_recv()
                        acc_s[0, :LONG] += dst[j].astype(jnp.float32)

            out[:, kv] = acc_s[0, :LONG].astype(jnp.bfloat16)

    sums(dv_out, dv_in, dv_recv, dv_o)
    sums(dk_out, dk_in, dk_recv, dk_o)
    dq_copy.wait_recv()
    for h in range(KV):

        @pl.when(mine != h)
        def _():
            dq_o[:, h * QW : (h + 1) * QW] = dq_in[...]


def write_results(*refs):
    sem = refs[12]
    copies = [pltpu.make_async_copy(refs[i], refs[6 + i], sem.at[i]) for i in range(6)]
    for copy in copies:
        copy.start()
    for copy in copies:
        copy.wait()


def on_device(lq, lk, lv, ldo, sq, sk, sv, sdo, lens):
    bf, f32 = jnp.bfloat16, jnp.float32
    args = (lq[0], lk[0], lv[0], ldo[0], sq[0], sk[0], sv[0], sdo[0], lens)
    kv, qw = KV * HEAD, KV * GROUP * HEAD
    shapes = [(LONG, qw), (LONG, kv), (LONG, kv), (SHORT, qw), (SHORT, kv), (SHORT, kv)]
    any_spec = pl.BlockSpec(memory_space=pltpu.HBM)
    vmem_spec = pl.BlockSpec(memory_space=pltpu.VMEM)
    outs = pl.pallas_call(
        kernel,
        out_shape=[pltpu.VMEM(s, bf) for s in shapes],
        in_specs=[any_spec] * 9,
        out_specs=[vmem_spec] * 6,
        scratch_shapes=[
            pltpu.VMEM((SHORT, qw), bf),
            pltpu.VMEM((SHORT, kv), bf),
            pltpu.VMEM((SHORT, kv), bf),
            pltpu.VMEM((SHORT, qw), bf),
            pltpu.VMEM((KV, LONG, QW), bf),
            pltpu.VMEM((KV, LONG, QW), bf),
            pltpu.VMEM((KV, ROWS, HEAD), bf),
            pltpu.VMEM((KV, ROWS, HEAD), bf),
            pltpu.VMEM((N, LONG, HEAD), bf),
            pltpu.VMEM((N, LONG, HEAD), bf),
            pltpu.VMEM((KV, PER, CHUNK, ROWS), f32),
            pltpu.VMEM((KV, PER, CHUNK, ROWS), f32),
            pltpu.VMEM((KV, PER, CHUNK, ROWS), bf),
            pltpu.VMEM((KV, PER, 1, ROWS), f32),
            pltpu.VMEM((KV, 1, ROWS), f32),
            pltpu.VMEM((PER, CHUNK, HEAD), f32),
            pltpu.VMEM((N, LONG, HEAD), bf),
            pltpu.VMEM((N, LONG, HEAD), bf),
            pltpu.VMEM((N, LONG, HEAD), bf),
            pltpu.VMEM((N, LONG, HEAD), bf),
            pltpu.VMEM((LONG, QW), bf),
            pltpu.VMEM((LONG, QW), bf),
            pltpu.SMEM((1, 1, DOCS), jnp.int32),
            pltpu.SemaphoreType.DMA((9,)),
        ]
        + [pltpu.SemaphoreType.DMA((n,)) for n in (PER, N, N) * 2 + (N,) * 4 + (2,) * 3],
        compiler_params=pltpu.CompilerParams(
            collective_id=0, has_side_effects=True, vmem_limit_bytes=40 << 20
        ),
        name="attention_grads",
    )(*(pltpu.with_memory_space_constraint(a, pltpu.HBM) for a in args))
    outs = pl.pallas_call(
        write_results,
        out_shape=[jax.ShapeDtypeStruct(s, bf) for s in shapes],
        in_specs=[vmem_spec] * 6,
        out_specs=[any_spec] * 6,
        scratch_shapes=[pltpu.SemaphoreType.DMA((6,))],
        compiler_params=pltpu.CompilerParams(vmem_limit_bytes=1 << 20),
        name="write_results",
    )(*(pltpu.with_memory_space_constraint(o, pltpu.VMEM) for o in outs))
    return tuple(o[None] for o in outs)


def solution(mesh):
    spec = P("dp", "context", "head")
    return jax.shard_map(
        on_device,
        mesh=mesh,
        in_specs=(spec,) * 8 + (P("dp", "context", None),),
        out_specs=(spec,) * 6,
        check_vma=False,
    )
```

```python
import functools
import math

import jax
import jax.numpy as jnp
from jax import lax
from jax.experimental import pallas as pl
from jax.experimental.pallas import tpu as pltpu
from jax.sharding import PartitionSpec as P

HEAD = 128
KV = 2
GROUP = 8
LONG = 64
SHORT = 128
SEG = 32
DOCS = 7
N = 16
PER = 4
CHUNK = PER * LONG
ROWS = GROUP * LONG
QW = GROUP * HEAD
MESH = pl.DeviceIdType.MESH
SCALE = 1.0 / math.sqrt(HEAD)
SCALE2 = SCALE * math.log2(math.e)
NEG = -1e30
NT = (((1,), (1,)), ((), ()))
TN = (((0,), (0,)), ((), ()))


def nt(a, b):
    return lax.dot_general(a, b, NT, preferred_element_type=jnp.float32)


def tn(a, b):
    return lax.dot_general(a, b, TN, preferred_element_type=jnp.float32)


def nn(a, b):
    return jnp.dot(a, b, preferred_element_type=jnp.float32)


def kernel(
    lq,
    lk,
    lv,
    ldo,
    sq,
    sk,
    sv,
    sdo,
    lens_hbm,
    dq_o,
    dk_o,
    dv_o,
    sdq_o,
    sdk_o,
    sdv_o,
    sq_in,
    sk_in,
    sv_in,
    sdo_in,
    q_in,
    do_in,
    q_s,
    do_s,
    k_all,
    v_all,
    e_s,
    gp_s,
    gs_s,
    w_s,
    d_s,
    acc_s,
    dv_out,
    dk_out,
    dv_in,
    dk_in,
    dq_out,
    dq_in,
    lens,
    in_sem,
    k_send_x,
    k_send_z,
    k_recv,
    v_send_x,
    v_send_z,
    v_recv,
    dv_send,
    dv_recv,
    dk_send,
    dk_recv,
    q_sem,
    do_sem,
    dq_sem,
):
    me = lax.axis_index("context")
    dp = lax.axis_index("dp")
    hd = lax.axis_index("head")
    x = me // PER
    z = me % PER
    crossed = hd == 0

    def partner_of(r):
        return jnp.where(crossed, PER - 1 - r, r + 1 - 2 * (r % 2))

    def head_of(r):
        return (r > partner_of(r)).astype(jnp.int32)

    def last_of(r):
        return jnp.maximum(r, partner_of(r))

    mine = head_of(x)
    other = 1 - mine
    high = last_of(x)
    low = jnp.minimum(x, partner_of(x))
    partner = partner_of(x) * PER + z
    kv_mine = pl.ds(pl.multiple_of(mine * HEAD, HEAD), HEAD)
    q_mine = pl.ds(pl.multiple_of(mine * QW, QW), QW)
    q_other = pl.ds(pl.multiple_of(other * QW, QW), QW)

    def dev(j):
        return (dp, j, hd)

    barrier = pltpu.get_barrier_semaphore()
    for d in range(1, N):
        pl.semaphore_signal(
            barrier, inc=1, device_id=dev(lax.rem(me + d, N)), device_id_type=MESH
        )

    loads = [
        pltpu.make_async_copy(src, dst, in_sem.at[i])
        for i, (src, dst) in enumerate(
            (
                (lk.at[:, kv_mine], k_all.at[me]),
                (lv.at[:, kv_mine], v_all.at[me]),
                (sq, sq_in),
                (sk, sk_in),
                (sdo, sdo_in),
                (sv, sv_in),
                (lens_hbm, lens),
                (lq.at[:, q_mine], q_in.at[mine]),
                (ldo.at[:, q_mine], do_in.at[mine]),
            )
        )
    ]
    for load in loads:
        load.start()
    for b in range(PER):

        @pl.when(b > z)
        def _():
            k_all[high * PER + b] = jnp.zeros((LONG, HEAD), jnp.bfloat16)
            v_all[high * PER + b] = jnp.zeros((LONG, HEAD), jnp.bfloat16)

    pl.semaphore_wait(barrier, N - 1)

    def copy(src, dst, send, recv, j):
        return pltpu.make_async_remote_copy(src, dst, send, recv, dev(j), MESH)

    def along_x(src, dst, send, recv):
        for r in range(PER):
            h = pl.ds(pl.multiple_of(head_of(r) * HEAD, HEAD), HEAD)
            yield (
                (x != r) & (x <= last_of(r)),
                copy(src.at[:, h], dst.at[me], send.at[r], recv.at[me], r * PER + z),
            )

    def along_z(src, dst, send, recv, b):
        for d in range(PER):
            yield (
                (z != d) & ((b < high) | ((b == high) & (d > z))),
                copy(
                    src,
                    dst.at[b * PER + z],
                    send.at[b * PER + d],
                    recv.at[b * PER + z],
                    x * PER + d,
                ),
            )

    def to_all(src, dst, send, recv):
        for r in (3, 2, 1, 0):
            h = pl.ds(pl.multiple_of(head_of(r) * HEAD, HEAD), HEAD)
            for d in range(PER):
                j = r * PER + d
                yield (
                    (me != j) & ((x < last_of(r)) | ((x == last_of(r)) & (z <= d))),
                    copy(src.at[:, h], dst.at[me], send.at[j], recv.at[me], j),
                )

    def wait_direct(dst, recv, b):
        for d in range(PER):
            j = b * PER + d

            @pl.when((me != j) & ((b < high) | ((b == high) & (d <= z))))
            def _():
                copy(dst.at[me], dst.at[j], recv.at[j], recv.at[j], me).wait_recv()

    def each(copies, act):
        for on, c in copies:

            @pl.when(on)
            def _():
                act(c)

    def start(c):
        c.start()

    def forward(dst, send_z, recv):
        for b in range(PER):

            @pl.when((x != b) & (b <= high))
            def _():
                copy(
                    dst.at[me], dst.at[b * PER + z], send_z.at[0], recv.at[b * PER + z], me
                ).wait_recv()
                each(along_z(dst.at[b * PER + z], dst, send_z, recv, b), start)

    def wait_row(dst, recv, b):
        for d in range(PER):

            @pl.when((z != d) & ((b < high) | ((b == high) & (d < z))))
            def _():
                copy(
                    dst.at[me], dst.at[b * PER + d], recv.at[b * PER + d], recv.at[b * PER + d], me
                ).wait_recv()

    def q_copy(src, dst, sem):
        return copy(src.at[:, q_other], dst.at[mine], sem.at[0], sem.at[1], partner)

    each(along_x(lv, v_all, v_send_x, v_recv), start)
    each(to_all(lk, k_all, k_send_z, k_recv), start)
    each(along_z(lv.at[:, kv_mine], v_all, v_send_z, v_recv, x), start)
    q_copy(lq, q_in, q_sem).start()
    q_copy(ldo, do_in, do_sem).start()

    for i in (2, 3, 4, 5, 6):
        loads[i].wait()
    ends = []
    total = jnp.int32(0)
    for i in range(DOCS):
        total = total + lens[0, 0, i]
        ends.append(total)
    outs = []
    for seg in range(SHORT // SEG):
        base = seg * SEG
        key_pos = base + lax.broadcasted_iota(jnp.int32, (SEG, GROUP * SEG), 0)
        query_pos = base + lax.rem(
            lax.broadcasted_iota(jnp.int32, (SEG, GROUP * SEG), 1), SEG
        )
        key_doc = jnp.zeros((SEG, GROUP * SEG), jnp.int32)
        query_doc = jnp.zeros((SEG, GROUP * SEG), jnp.int32)
        for end in ends:
            key_doc = key_doc + (key_pos >= end).astype(jnp.int32)
            query_doc = query_doc + (query_pos >= end).astype(jnp.int32)
        allowed = (key_doc == query_doc) & (key_pos <= query_pos)
        rows = slice(base, base + SEG)
        for h in range(KV):
            kv = slice(h * HEAD, (h + 1) * HEAD)
            cols = [
                slice((h * GROUP + g) * HEAD, (h * GROUP + g + 1) * HEAD)
                for g in range(GROUP)
            ]
            q = jnp.concatenate([sq_in[rows, c] for c in cols], axis=0)
            do = jnp.concatenate([sdo_in[rows, c] for c in cols], axis=0)
            k = sk_in[rows, kv]
            v = sv_in[rows, kv]
            s = jnp.where(allowed, nt(k, q), NEG)
            e = jnp.exp2((s - jnp.max(s, axis=0, keepdims=True)) * SCALE2)
            p = e * (1.0 / jnp.sum(e, axis=0, keepdims=True))
            gp = nt(v, do)
            delta = jnp.sum(p * gp, axis=0, keepdims=True)
            gs = (p * (gp - delta)).astype(jnp.bfloat16)
            sdv_o[rows, kv] = nn(p.astype(jnp.bfloat16), do).astype(jnp.bfloat16)
            sdk_o[rows, kv] = (nn(gs, q) * SCALE).astype(jnp.bfloat16)
            dq = (tn(gs, k) * SCALE).astype(jnp.bfloat16)
            for g, c in enumerate(cols):
                sdq_o[rows, c] = dq[g * SEG : (g + 1) * SEG]

    for i in (0, 1):
        loads[i].wait()
    forward(v_all, v_send_z, v_recv)

    def spread(src, dst, p):
        for g in range(GROUP):
            dst[p, g * LONG : (g + 1) * LONG] = src[p, :, g * HEAD : (g + 1) * HEAD]

    offset = lax.broadcasted_iota(jnp.int32, (CHUNK, ROWS), 0) - lax.rem(
        lax.broadcasted_iota(jnp.int32, (CHUNK, ROWS), 1), LONG
    )
    def by_count(p, act):
        for n in range(1 + p, PER + p):

            @pl.when((low, high)[p] == n - 1)
            def _():
                act(p, n)

    def by_pair(act):
        for few, many in ((1, 4), (2, 3), (1, 2), (3, 4)):

            @pl.when((low == few - 1) & (high == many - 1))
            def _():
                act(few, many)

    def keys_of(ref, c, n=1):
        return ref[c * PER : (c + n) * PER].reshape(n * CHUNK, HEAD)

    def scores(p, n):
        tops = []
        sums = []
        for c in range(n):
            s = nt(keys_of(k_all, c), q_s[p])
            if c == n - 1:
                s = jnp.where(offset <= z * LONG, s, NEG)
            m = jnp.max(s, axis=0, keepdims=True)
            e = jnp.exp2((s - m) * SCALE2)
            e_s[p, c] = e
            tops.append(m)
            sums.append(jnp.sum(e, axis=0, keepdims=True))
        top = tops[0]
        for m in tops[1:]:
            top = jnp.maximum(top, m)
        factors = [jnp.exp2((m - top) * SCALE2) for m in tops]
        total = factors[0] * sums[0]
        for c in range(1, n):
            total = total + factors[c] * sums[c]
        inverse = 1.0 / total
        for c in range(n):
            w_s[p, c] = factors[c] * inverse

    def grad_copy(src, dst, send, recv, b, d):
        j = b * PER + d
        return copy(src.at[j], dst.at[me], send.at[j], recv.at[me], j)

    def is_sent(b, d):
        return (me != b * PER + d) & ((b < high) | ((b == high) & (d <= z)))

    def send_chunk(total, src, dst, send, recv, b):
        part = total.astype(jnp.bfloat16).reshape(PER, LONG, HEAD)
        src[pl.ds(b * PER, PER)] = part
        for d in range(PER):

            @pl.when(is_sent(b, d))
            def _():
                grad_copy(src, dst, send, recv, b, d).start()

    def shares(product, dst, few, many):
        for c in range(many):
            total = product(1, c)
            if c < few:
                total = total + product(0, c)
            send_chunk(total, *dst, c)

    def value_product(p, c):
        return nn((e_s[p, c] * w_s[p, c]).astype(jnp.bfloat16), do_s[p])

    def key_product(p, c):
        gs = (e_s[p, c] * (w_s[p, c] * (gp_s[p, c] - d_s[p]))).astype(jnp.bfloat16)
        gs_s[p, c] = gs
        return nn(gs, q_s[p]) * SCALE

    def prob_grads(p, n):
        delta = jnp.zeros((1, ROWS), jnp.float32)
        for c in range(n):
            gp = nt(keys_of(v_all, c), do_s[p])
            gp_s[p, c] = gp
            delta = delta + w_s[p, c] * jnp.sum(e_s[p, c] * gp, axis=0, keepdims=True)
        d_s[p] = delta

    def query_grads(p, n):
        gs = gs_s[p, :n].reshape(n * CHUNK, ROWS)
        return (tn(gs, keys_of(k_all, 0, n)) * SCALE).astype(jnp.bfloat16)

    dv_ends = (dv_out, dv_in, dv_send, dv_recv)
    dk_ends = (dk_out, dk_in, dk_send, dk_recv)
    loads[7].wait()
    spread(q_in, q_s, mine)
    q_copy(lq, q_in, q_sem).wait_recv()
    spread(q_in, q_s, other)
    for b in range(PER):
        wait_direct(k_all, k_recv, b)

    def both_scores(few, many):
        scores(0, few)
        scores(1, many)

    by_pair(both_scores)
    loads[8].wait()
    spread(do_in, do_s, mine)
    q_copy(ldo, do_in, do_sem).wait_recv()
    spread(do_in, do_s, other)
    by_pair(functools.partial(shares, value_product, dv_ends))
    for b in range(PER):
        wait_row(v_all, v_recv, b)

    def both_key_grads(few, many):
        prob_grads(0, few)
        prob_grads(1, many)
        shares(key_product, dk_ends, few, many)

    by_pair(both_key_grads)

    def store_query_grads(p, n):
        grad = query_grads(p, n)
        for g in range(GROUP):
            dq_out[p, :, g * HEAD : (g + 1) * HEAD] = grad[g * LONG : (g + 1) * LONG]

    dq_copy = copy(dq_out.at[other], dq_in, dq_sem.at[0], dq_sem.at[1], partner)
    for p in range(KV):
        by_count(p, store_query_grads)
        pl.when(other == p)(dq_copy.start)
    for h in range(KV):

        @pl.when(mine == h)
        def _():
            dq_o[:, h * QW : (h + 1) * QW] = dq_out[mine]

    def wait_send(c):
        c.wait_send()

    each(to_all(lk, k_all, k_send_z, k_recv), wait_send)
    each(along_x(lv, v_all, v_send_x, v_recv), wait_send)
    for b in range(PER):
        each(along_z(v_all.at[b * PER + z], v_all, v_send_z, v_recv, b), wait_send)
        for d in range(PER):

            @pl.when(is_sent(b, d))
            def _():
                grad_copy(dv_out, dv_in, dv_send, dv_recv, b, d).wait_send()
                grad_copy(dk_out, dk_in, dk_send, dk_recv, b, d).wait_send()

    q_copy(lq, q_in, q_sem).wait_send()
    q_copy(ldo, do_in, do_sem).wait_send()
    dq_copy.wait_send()

    def sums(src, dst, recv, out):
        for h in range(KV):
            kv = slice(h * HEAD, (h + 1) * HEAD)

            @pl.when(mine == h)
            def _():
                acc_s[0] = src[me].astype(jnp.float32)

            @pl.when(mine != h)
            def _():
                acc_s[0] = jnp.zeros((LONG, HEAD), jnp.float32)

            for i in range(2):
                r = jnp.where(crossed, 2 * h + i, 2 * i + h)
                last = last_of(r)
                for d in range(PER):
                    j = r * PER + d

                    @pl.when((me != j) & ((x < last) | ((x == last) & (z <= d))))
                    def _():
                        copy(src.at[me], dst.at[j], recv.at[j], recv.at[j], me).wait_recv()
                        acc_s[0] += dst[j].astype(jnp.float32)

            out[:, kv] = acc_s[0].astype(jnp.bfloat16)

    sums(dv_out, dv_in, dv_recv, dv_o)
    sums(dk_out, dk_in, dk_recv, dk_o)
    dq_copy.wait_recv()
    for h in range(KV):

        @pl.when(mine != h)
        def _():
            dq_o[:, h * QW : (h + 1) * QW] = dq_in[...]


def write_results(*refs):
    sem = refs[12]
    copies = [pltpu.make_async_copy(refs[i], refs[6 + i], sem.at[i]) for i in range(6)]
    for copy in copies:
        copy.start()
    for copy in copies:
        copy.wait()


def on_device(lq, lk, lv, ldo, sq, sk, sv, sdo, lens):
    bf, f32 = jnp.bfloat16, jnp.float32
    args = (lq[0], lk[0], lv[0], ldo[0], sq[0], sk[0], sv[0], sdo[0], lens)
    kv, qw = KV * HEAD, KV * GROUP * HEAD
    shapes = [(LONG, qw), (LONG, kv), (LONG, kv), (SHORT, qw), (SHORT, kv), (SHORT, kv)]
    any_spec = pl.BlockSpec(memory_space=pltpu.HBM)
    vmem_spec = pl.BlockSpec(memory_space=pltpu.VMEM)
    outs = pl.pallas_call(
        kernel,
        out_shape=[pltpu.VMEM(s, bf) for s in shapes],
        in_specs=[any_spec] * 9,
        out_specs=[vmem_spec] * 6,
        scratch_shapes=[
            pltpu.VMEM((SHORT, qw), bf),
            pltpu.VMEM((SHORT, kv), bf),
            pltpu.VMEM((SHORT, kv), bf),
            pltpu.VMEM((SHORT, qw), bf),
            pltpu.VMEM((KV, LONG, QW), bf),
            pltpu.VMEM((KV, LONG, QW), bf),
            pltpu.VMEM((KV, ROWS, HEAD), bf),
            pltpu.VMEM((KV, ROWS, HEAD), bf),
            pltpu.VMEM((N, LONG, HEAD), bf),
            pltpu.VMEM((N, LONG, HEAD), bf),
            pltpu.VMEM((KV, PER, CHUNK, ROWS), f32),
            pltpu.VMEM((KV, PER, CHUNK, ROWS), f32),
            pltpu.VMEM((KV, PER, CHUNK, ROWS), bf),
            pltpu.VMEM((KV, PER, 1, ROWS), f32),
            pltpu.VMEM((KV, 1, ROWS), f32),
            pltpu.VMEM((1, LONG, HEAD), f32),
            pltpu.VMEM((N, LONG, HEAD), bf),
            pltpu.VMEM((N, LONG, HEAD), bf),
            pltpu.VMEM((N, LONG, HEAD), bf),
            pltpu.VMEM((N, LONG, HEAD), bf),
            pltpu.VMEM((KV, LONG, QW), bf),
            pltpu.VMEM((LONG, QW), bf),
            pltpu.SMEM((1, 1, DOCS), jnp.int32),
            pltpu.SemaphoreType.DMA((9,)),
        ]
        + [pltpu.SemaphoreType.DMA((n,)) for n in (PER, N, N) * 2 + (N,) * 4 + (2,) * 3],
        compiler_params=pltpu.CompilerParams(
            collective_id=0, has_side_effects=True, vmem_limit_bytes=40 << 20
        ),
        name="attention_grads",
    )(*(pltpu.with_memory_space_constraint(a, pltpu.HBM) for a in args))
    outs = pl.pallas_call(
        write_results,
        out_shape=[jax.ShapeDtypeStruct(s, bf) for s in shapes],
        in_specs=[vmem_spec] * 6,
        out_specs=[any_spec] * 6,
        scratch_shapes=[pltpu.SemaphoreType.DMA((6,))],
        compiler_params=pltpu.CompilerParams(vmem_limit_bytes=1 << 20),
        name="write_results",
    )(*(pltpu.with_memory_space_constraint(o, pltpu.VMEM) for o in outs))
    return tuple(o[None] for o in outs)


def solution(mesh):
    spec = P("dp", "context", "head")
    return jax.shard_map(
        on_device,
        mesh=mesh,
        in_specs=(spec,) * 8 + (P("dp", "context", None),),
        out_specs=(spec,) * 6,
        check_vma=False,
    )
```

```python
import functools
import math

import jax
import jax.numpy as jnp
from jax import lax
from jax.experimental import pallas as pl
from jax.experimental.pallas import tpu as pltpu
from jax.sharding import PartitionSpec as P

HEAD = 128
KV = 2
GROUP = 8
LONG = 64
SHORT = 128
SEG = 32
DOCS = 7
N = 16
PER = 4
CHUNK = PER * LONG
ROWS = GROUP * LONG
QW = GROUP * HEAD
MESH = pl.DeviceIdType.MESH
SCALE = 1.0 / math.sqrt(HEAD)
SCALE2 = SCALE * math.log2(math.e)
NEG = -1e30
NT = (((1,), (1,)), ((), ()))
TN = (((0,), (0,)), ((), ()))


def nt(a, b):
    return lax.dot_general(a, b, NT, preferred_element_type=jnp.float32)


def tn(a, b):
    return lax.dot_general(a, b, TN, preferred_element_type=jnp.float32)


def nn(a, b):
    return jnp.dot(a, b, preferred_element_type=jnp.float32)


def kernel(
    lq,
    lk,
    lv,
    ldo,
    sq,
    sk,
    sv,
    sdo,
    lens_hbm,
    dq_o,
    dk_o,
    dv_o,
    sdq_o,
    sdk_o,
    sdv_o,
    sq_in,
    sk_in,
    sv_in,
    sdo_in,
    q_in,
    do_in,
    q_s,
    do_s,
    k_all,
    v_all,
    e_s,
    gp_s,
    gs_s,
    w_s,
    d_s,
    acc_s,
    dv_out,
    dk_out,
    dv_in,
    dk_in,
    dq_out,
    dq_in,
    lens,
    in_sem,
    k_send_x,
    k_send_z,
    k_recv,
    v_send_x,
    v_send_z,
    v_recv,
    dv_send,
    dv_recv,
    dk_send,
    dk_recv,
    q_sem,
    do_sem,
    dq_sem,
):
    me = lax.axis_index("context")
    dp = lax.axis_index("dp")
    hd = lax.axis_index("head")
    x = me // PER
    z = me % PER
    crossed = hd == 0

    def partner_of(r):
        return jnp.where(crossed, PER - 1 - r, r + 1 - 2 * (r % 2))

    def head_of(r):
        return (r > partner_of(r)).astype(jnp.int32)

    def last_of(r):
        return jnp.maximum(r, partner_of(r))

    mine = head_of(x)
    other = 1 - mine
    high = last_of(x)
    low = jnp.minimum(x, partner_of(x))
    partner = partner_of(x) * PER + z
    kv_mine = pl.ds(pl.multiple_of(mine * HEAD, HEAD), HEAD)
    q_mine = pl.ds(pl.multiple_of(mine * QW, QW), QW)
    q_other = pl.ds(pl.multiple_of(other * QW, QW), QW)

    def dev(j):
        return (dp, j, hd)

    barrier = pltpu.get_barrier_semaphore()
    for d in range(1, N):
        pl.semaphore_signal(
            barrier, inc=1, device_id=dev(lax.rem(me + d, N)), device_id_type=MESH
        )

    loads = [
        pltpu.make_async_copy(src, dst, in_sem.at[i])
        for i, (src, dst) in enumerate(
            (
                (lk.at[:, kv_mine], k_all.at[me]),
                (lv.at[:, kv_mine], v_all.at[me]),
                (sq, sq_in),
                (sk, sk_in),
                (sdo, sdo_in),
                (sv, sv_in),
                (lens_hbm, lens),
                (lq.at[:, q_mine], q_in.at[mine]),
                (ldo.at[:, q_mine], do_in.at[mine]),
            )
        )
    ]
    for load in loads:
        load.start()
    for b in range(PER):

        @pl.when(b > z)
        def _():
            k_all[high * PER + b] = jnp.zeros((LONG, HEAD), jnp.bfloat16)
            v_all[high * PER + b] = jnp.zeros((LONG, HEAD), jnp.bfloat16)

    pl.semaphore_wait(barrier, N - 1)

    def copy(src, dst, send, recv, j):
        return pltpu.make_async_remote_copy(src, dst, send, recv, dev(j), MESH)

    def along_x(src, dst, send, recv):
        for r in range(PER):
            h = pl.ds(pl.multiple_of(head_of(r) * HEAD, HEAD), HEAD)
            yield (
                (x != r) & (x <= last_of(r)),
                copy(src.at[:, h], dst.at[me], send.at[r], recv.at[me], r * PER + z),
            )

    def along_z(src, dst, send, recv, b):
        for d in range(PER):
            yield (
                (z != d) & ((b < high) | ((b == high) & (d > z))),
                copy(
                    src,
                    dst.at[b * PER + z],
                    send.at[b * PER + d],
                    recv.at[b * PER + z],
                    x * PER + d,
                ),
            )

    def to_all(src, dst, send, recv):
        for r in (3, 2, 1, 0):
            h = pl.ds(pl.multiple_of(head_of(r) * HEAD, HEAD), HEAD)
            for d in range(PER):
                j = r * PER + d
                yield (
                    (me != j) & ((x < last_of(r)) | ((x == last_of(r)) & (z <= d))),
                    copy(src.at[:, h], dst.at[me], send.at[j], recv.at[me], j),
                )

    def wait_direct(dst, recv, b):
        for d in range(PER):
            j = b * PER + d

            @pl.when((me != j) & ((b < high) | ((b == high) & (d <= z))))
            def _():
                copy(dst.at[me], dst.at[j], recv.at[j], recv.at[j], me).wait_recv()

    def each(copies, act):
        for on, c in copies:

            @pl.when(on)
            def _():
                act(c)

    def start(c):
        c.start()

    def forward(dst, send_z, recv):
        for b in range(PER):

            @pl.when((x != b) & (b <= high))
            def _():
                copy(
                    dst.at[me], dst.at[b * PER + z], send_z.at[0], recv.at[b * PER + z], me
                ).wait_recv()
                each(along_z(dst.at[b * PER + z], dst, send_z, recv, b), start)

    def wait_row(dst, recv, b):
        for d in range(PER):

            @pl.when((z != d) & ((b < high) | ((b == high) & (d < z))))
            def _():
                copy(
                    dst.at[me], dst.at[b * PER + d], recv.at[b * PER + d], recv.at[b * PER + d], me
                ).wait_recv()

    def q_copy(src, dst, sem):
        return copy(src.at[:, q_other], dst.at[mine], sem.at[0], sem.at[1], partner)

    each(along_x(lv, v_all, v_send_x, v_recv), start)
    each(to_all(lk, k_all, k_send_z, k_recv), start)
    each(along_z(lv.at[:, kv_mine], v_all, v_send_z, v_recv, x), start)
    q_copy(lq, q_in, q_sem).start()
    q_copy(ldo, do_in, do_sem).start()

    for i in (0, 1):
        loads[i].wait()
    forward(v_all, v_send_z, v_recv)

    def spread(src, dst, p):
        for g in range(GROUP):
            dst[p, g * LONG : (g + 1) * LONG] = src[p, :, g * HEAD : (g + 1) * HEAD]

    offset = lax.broadcasted_iota(jnp.int32, (CHUNK, ROWS), 0) - lax.rem(
        lax.broadcasted_iota(jnp.int32, (CHUNK, ROWS), 1), LONG
    )
    def by_count(p, act):
        for n in range(1 + p, PER + p):

            @pl.when((low, high)[p] == n - 1)
            def _():
                act(p, n)

    def by_pair(act):
        for few, many in ((1, 4), (2, 3), (1, 2), (3, 4)):

            @pl.when((low == few - 1) & (high == many - 1))
            def _():
                act(few, many)

    def keys_of(ref, c, n=1):
        return ref[c * PER : (c + n) * PER].reshape(n * CHUNK, HEAD)

    def scores(p, n):
        tops = []
        sums = []
        for c in range(n):
            s = nt(keys_of(k_all, c), q_s[p])
            if c == n - 1:
                s = jnp.where(offset <= z * LONG, s, NEG)
            m = jnp.max(s, axis=0, keepdims=True)
            e = jnp.exp2((s - m) * SCALE2)
            e_s[p, c] = e
            tops.append(m)
            sums.append(jnp.sum(e, axis=0, keepdims=True))
        top = tops[0]
        for m in tops[1:]:
            top = jnp.maximum(top, m)
        factors = [jnp.exp2((m - top) * SCALE2) for m in tops]
        total = factors[0] * sums[0]
        for c in range(1, n):
            total = total + factors[c] * sums[c]
        inverse = 1.0 / total
        for c in range(n):
            w_s[p, c] = factors[c] * inverse

    def grad_copy(src, dst, send, recv, b, d):
        j = b * PER + d
        return copy(src.at[j], dst.at[me], send.at[j], recv.at[me], j)

    def is_sent(b, d):
        return (me != b * PER + d) & ((b < high) | ((b == high) & (d <= z)))

    def send_chunk(total, src, dst, send, recv, b):
        part = total.astype(jnp.bfloat16).reshape(PER, LONG, HEAD)
        src[pl.ds(b * PER, PER)] = part
        for d in range(PER):

            @pl.when(is_sent(b, d))
            def _():
                grad_copy(src, dst, send, recv, b, d).start()

    def shares(product, dst, few, many):
        for c in range(many):
            total = product(1, c)
            if c < few:
                total = total + product(0, c)
            send_chunk(total, *dst, c)

    def value_product(p, c):
        return nn((e_s[p, c] * w_s[p, c]).astype(jnp.bfloat16), do_s[p])

    def key_product(p, c):
        gs = (e_s[p, c] * (w_s[p, c] * (gp_s[p, c] - d_s[p]))).astype(jnp.bfloat16)
        gs_s[p, c] = gs
        return nn(gs, q_s[p]) * SCALE

    def prob_grads(p, n):
        delta = jnp.zeros((1, ROWS), jnp.float32)
        for c in range(n):
            gp = nt(keys_of(v_all, c), do_s[p])
            gp_s[p, c] = gp
            delta = delta + w_s[p, c] * jnp.sum(e_s[p, c] * gp, axis=0, keepdims=True)
        d_s[p] = delta

    def query_grads(p, n):
        gs = gs_s[p, :n].reshape(n * CHUNK, ROWS)
        return (tn(gs, keys_of(k_all, 0, n)) * SCALE).astype(jnp.bfloat16)

    dv_ends = (dv_out, dv_in, dv_send, dv_recv)
    dk_ends = (dk_out, dk_in, dk_send, dk_recv)
    loads[7].wait()
    spread(q_in, q_s, mine)
    q_copy(lq, q_in, q_sem).wait_recv()
    spread(q_in, q_s, other)
    for b in range(PER):
        wait_direct(k_all, k_recv, b)

    def both_scores(few, many):
        scores(0, few)
        scores(1, many)

    by_pair(both_scores)
    loads[8].wait()
    spread(do_in, do_s, mine)
    q_copy(ldo, do_in, do_sem).wait_recv()
    spread(do_in, do_s, other)
    by_pair(functools.partial(shares, value_product, dv_ends))
    for b in range(PER):
        wait_row(v_all, v_recv, b)

    def both_key_grads(few, many):
        prob_grads(0, few)
        prob_grads(1, many)
        shares(key_product, dk_ends, few, many)

    by_pair(both_key_grads)

    def store_query_grads(p, n):
        grad = query_grads(p, n)
        for g in range(GROUP):
            dq_out[p, :, g * HEAD : (g + 1) * HEAD] = grad[g * LONG : (g + 1) * LONG]

    dq_copy = copy(dq_out.at[other], dq_in, dq_sem.at[0], dq_sem.at[1], partner)
    for p in range(KV):
        by_count(p, store_query_grads)
        pl.when(other == p)(dq_copy.start)
    for h in range(KV):

        @pl.when(mine == h)
        def _():
            dq_o[:, h * QW : (h + 1) * QW] = dq_out[mine]

    for i in (2, 3, 4, 5, 6):
        loads[i].wait()
    ends = []
    total = jnp.int32(0)
    for i in range(DOCS):
        total = total + lens[0, 0, i]
        ends.append(total)
    outs = []
    for seg in range(SHORT // SEG):
        base = seg * SEG
        key_pos = base + lax.broadcasted_iota(jnp.int32, (SEG, GROUP * SEG), 0)
        query_pos = base + lax.rem(
            lax.broadcasted_iota(jnp.int32, (SEG, GROUP * SEG), 1), SEG
        )
        key_doc = jnp.zeros((SEG, GROUP * SEG), jnp.int32)
        query_doc = jnp.zeros((SEG, GROUP * SEG), jnp.int32)
        for end in ends:
            key_doc = key_doc + (key_pos >= end).astype(jnp.int32)
            query_doc = query_doc + (query_pos >= end).astype(jnp.int32)
        allowed = (key_doc == query_doc) & (key_pos <= query_pos)
        rows = slice(base, base + SEG)
        for h in range(KV):
            kv = slice(h * HEAD, (h + 1) * HEAD)
            cols = [
                slice((h * GROUP + g) * HEAD, (h * GROUP + g + 1) * HEAD)
                for g in range(GROUP)
            ]
            q = jnp.concatenate([sq_in[rows, c] for c in cols], axis=0)
            do = jnp.concatenate([sdo_in[rows, c] for c in cols], axis=0)
            k = sk_in[rows, kv]
            v = sv_in[rows, kv]
            s = jnp.where(allowed, nt(k, q), NEG)
            e = jnp.exp2((s - jnp.max(s, axis=0, keepdims=True)) * SCALE2)
            p = e * (1.0 / jnp.sum(e, axis=0, keepdims=True))
            gp = nt(v, do)
            delta = jnp.sum(p * gp, axis=0, keepdims=True)
            gs = (p * (gp - delta)).astype(jnp.bfloat16)
            sdv_o[rows, kv] = nn(p.astype(jnp.bfloat16), do).astype(jnp.bfloat16)
            sdk_o[rows, kv] = (nn(gs, q) * SCALE).astype(jnp.bfloat16)
            dq = (tn(gs, k) * SCALE).astype(jnp.bfloat16)
            for g, c in enumerate(cols):
                sdq_o[rows, c] = dq[g * SEG : (g + 1) * SEG]

    def wait_send(c):
        c.wait_send()

    each(to_all(lk, k_all, k_send_z, k_recv), wait_send)
    each(along_x(lv, v_all, v_send_x, v_recv), wait_send)
    for b in range(PER):
        each(along_z(v_all.at[b * PER + z], v_all, v_send_z, v_recv, b), wait_send)
        for d in range(PER):

            @pl.when(is_sent(b, d))
            def _():
                grad_copy(dv_out, dv_in, dv_send, dv_recv, b, d).wait_send()
                grad_copy(dk_out, dk_in, dk_send, dk_recv, b, d).wait_send()

    q_copy(lq, q_in, q_sem).wait_send()
    q_copy(ldo, do_in, do_sem).wait_send()
    dq_copy.wait_send()

    def sums(src, dst, recv, out):
        for h in range(KV):
            kv = slice(h * HEAD, (h + 1) * HEAD)

            @pl.when(mine == h)
            def _():
                acc_s[0] = src[me].astype(jnp.float32)

            @pl.when(mine != h)
            def _():
                acc_s[0] = jnp.zeros((LONG, HEAD), jnp.float32)

            for i in range(2):
                r = jnp.where(crossed, 2 * h + i, 2 * i + h)
                last = last_of(r)
                for d in range(PER):
                    j = r * PER + d

                    @pl.when((me != j) & ((x < last) | ((x == last) & (z <= d))))
                    def _():
                        copy(src.at[me], dst.at[j], recv.at[j], recv.at[j], me).wait_recv()
                        acc_s[0] += dst[j].astype(jnp.float32)

            out[:, kv] = acc_s[0].astype(jnp.bfloat16)

    sums(dv_out, dv_in, dv_recv, dv_o)
    sums(dk_out, dk_in, dk_recv, dk_o)
    dq_copy.wait_recv()
    for h in range(KV):

        @pl.when(mine != h)
        def _():
            dq_o[:, h * QW : (h + 1) * QW] = dq_in[...]


def write_results(*refs):
    sem = refs[12]
    copies = [pltpu.make_async_copy(refs[i], refs[6 + i], sem.at[i]) for i in range(6)]
    for copy in copies:
        copy.start()
    for copy in copies:
        copy.wait()


def on_device(lq, lk, lv, ldo, sq, sk, sv, sdo, lens):
    bf, f32 = jnp.bfloat16, jnp.float32
    args = (lq[0], lk[0], lv[0], ldo[0], sq[0], sk[0], sv[0], sdo[0], lens)
    kv, qw = KV * HEAD, KV * GROUP * HEAD
    shapes = [(LONG, qw), (LONG, kv), (LONG, kv), (SHORT, qw), (SHORT, kv), (SHORT, kv)]
    any_spec = pl.BlockSpec(memory_space=pltpu.HBM)
    vmem_spec = pl.BlockSpec(memory_space=pltpu.VMEM)
    outs = pl.pallas_call(
        kernel,
        out_shape=[pltpu.VMEM(s, bf) for s in shapes],
        in_specs=[any_spec] * 9,
        out_specs=[vmem_spec] * 6,
        scratch_shapes=[
            pltpu.VMEM((SHORT, qw), bf),
            pltpu.VMEM((SHORT, kv), bf),
            pltpu.VMEM((SHORT, kv), bf),
            pltpu.VMEM((SHORT, qw), bf),
            pltpu.VMEM((KV, LONG, QW), bf),
            pltpu.VMEM((KV, LONG, QW), bf),
            pltpu.VMEM((KV, ROWS, HEAD), bf),
            pltpu.VMEM((KV, ROWS, HEAD), bf),
            pltpu.VMEM((N, LONG, HEAD), bf),
            pltpu.VMEM((N, LONG, HEAD), bf),
            pltpu.VMEM((KV, PER, CHUNK, ROWS), f32),
            pltpu.VMEM((KV, PER, CHUNK, ROWS), f32),
            pltpu.VMEM((KV, PER, CHUNK, ROWS), bf),
            pltpu.VMEM((KV, PER, 1, ROWS), f32),
            pltpu.VMEM((KV, 1, ROWS), f32),
            pltpu.VMEM((1, LONG, HEAD), f32),
            pltpu.VMEM((N, LONG, HEAD), bf),
            pltpu.VMEM((N, LONG, HEAD), bf),
            pltpu.VMEM((N, LONG, HEAD), bf),
            pltpu.VMEM((N, LONG, HEAD), bf),
            pltpu.VMEM((KV, LONG, QW), bf),
            pltpu.VMEM((LONG, QW), bf),
            pltpu.SMEM((1, 1, DOCS), jnp.int32),
            pltpu.SemaphoreType.DMA((9,)),
        ]
        + [pltpu.SemaphoreType.DMA((n,)) for n in (PER, N, N) * 2 + (N,) * 4 + (2,) * 3],
        compiler_params=pltpu.CompilerParams(
            collective_id=0, has_side_effects=True, vmem_limit_bytes=40 << 20
        ),
        name="attention_grads",
    )(*(pltpu.with_memory_space_constraint(a, pltpu.HBM) for a in args))
    outs = pl.pallas_call(
        write_results,
        out_shape=[jax.ShapeDtypeStruct(s, bf) for s in shapes],
        in_specs=[vmem_spec] * 6,
        out_specs=[any_spec] * 6,
        scratch_shapes=[pltpu.SemaphoreType.DMA((6,))],
        compiler_params=pltpu.CompilerParams(vmem_limit_bytes=1 << 20),
        name="write_results",
    )(*(pltpu.with_memory_space_constraint(o, pltpu.VMEM) for o in outs))
    return tuple(o[None] for o in outs)


def solution(mesh):
    spec = P("dp", "context", "head")
    return jax.shard_map(
        on_device,
        mesh=mesh,
        in_specs=(spec,) * 8 + (P("dp", "context", None),),
        out_specs=(spec,) * 6,
        check_vma=False,
    )
```

```python
import functools
import math

import jax
import jax.numpy as jnp
from jax import lax
from jax.experimental import pallas as pl
from jax.experimental.pallas import tpu as pltpu
from jax.sharding import PartitionSpec as P

HEAD = 128
KV = 2
GROUP = 8
LONG = 64
SHORT = 128
SEG = 32
DOCS = 7
N = 16
PER = 4
CHUNK = PER * LONG
ROWS = GROUP * LONG
QW = GROUP * HEAD
MESH = pl.DeviceIdType.MESH
SCALE = 1.0 / math.sqrt(HEAD)
SCALE2 = SCALE * math.log2(math.e)
NEG = -1e30
NT = (((1,), (1,)), ((), ()))
TN = (((0,), (0,)), ((), ()))


def nt(a, b):
    return lax.dot_general(a, b, NT, preferred_element_type=jnp.float32)


def tn(a, b):
    return lax.dot_general(a, b, TN, preferred_element_type=jnp.float32)


def nn(a, b):
    return jnp.dot(a, b, preferred_element_type=jnp.float32)


def kernel(
    lq,
    lk,
    lv,
    ldo,
    sq,
    sk,
    sv,
    sdo,
    lens_hbm,
    dq_o,
    dk_o,
    dv_o,
    sdq_o,
    sdk_o,
    sdv_o,
    sq_in,
    sk_in,
    sv_in,
    sdo_in,
    q_in,
    do_in,
    q_s,
    do_s,
    k_all,
    v_all,
    e_s,
    gp_s,
    gs_s,
    w_s,
    d_s,
    acc_s,
    dv_out,
    dk_out,
    dv_in,
    dk_in,
    dq_out,
    dq_in,
    lens,
    in_sem,
    k_send_x,
    k_send_z,
    k_recv,
    v_send_x,
    v_send_z,
    v_recv,
    dv_send,
    dv_recv,
    dk_send,
    dk_recv,
    q_sem,
    do_sem,
    dq_sem,
):
    me = lax.axis_index("context")
    dp = lax.axis_index("dp")
    hd = lax.axis_index("head")
    x = me // PER
    z = me % PER
    crossed = hd == 0

    def partner_of(r):
        return jnp.where(crossed, PER - 1 - r, r + 1 - 2 * (r % 2))

    def head_of(r):
        return (r > partner_of(r)).astype(jnp.int32)

    def last_of(r):
        return jnp.maximum(r, partner_of(r))

    mine = head_of(x)
    other = 1 - mine
    high = last_of(x)
    low = jnp.minimum(x, partner_of(x))
    partner = partner_of(x) * PER + z
    kv_mine = pl.ds(pl.multiple_of(mine * HEAD, HEAD), HEAD)
    q_mine = pl.ds(pl.multiple_of(mine * QW, QW), QW)
    q_other = pl.ds(pl.multiple_of(other * QW, QW), QW)

    def dev(j):
        return (dp, j, hd)

    barrier = pltpu.get_barrier_semaphore()
    for d in range(1, N):
        pl.semaphore_signal(
            barrier, inc=1, device_id=dev(lax.rem(me + d, N)), device_id_type=MESH
        )

    loads = [
        pltpu.make_async_copy(src, dst, in_sem.at[i])
        for i, (src, dst) in enumerate(
            (
                (lk.at[:, kv_mine], k_all.at[me]),
                (lv.at[:, kv_mine], v_all.at[me]),
                (sq, sq_in),
                (sk, sk_in),
                (sdo, sdo_in),
                (sv, sv_in),
                (lens_hbm, lens),
                (lq.at[:, q_mine], q_in.at[mine]),
                (ldo.at[:, q_mine], do_in.at[mine]),
            )
        )
    ]
    for load in loads:
        load.start()
    for b in range(PER):

        @pl.when(b > z)
        def _():
            k_all[high * PER + b] = jnp.zeros((LONG, HEAD), jnp.bfloat16)
            v_all[high * PER + b] = jnp.zeros((LONG, HEAD), jnp.bfloat16)

    pl.semaphore_wait(barrier, N - 1)

    def copy(src, dst, send, recv, j):
        return pltpu.make_async_remote_copy(src, dst, send, recv, dev(j), MESH)

    def along_x(src, dst, send, recv):
        for r in range(PER):
            h = pl.ds(pl.multiple_of(head_of(r) * HEAD, HEAD), HEAD)
            yield (
                (x != r) & (x <= last_of(r)),
                copy(src.at[:, h], dst.at[me], send.at[r], recv.at[me], r * PER + z),
            )

    def along_z(src, dst, send, recv, b):
        for d in range(PER):
            yield (
                (z != d) & ((b < high) | ((b == high) & (d > z))),
                copy(
                    src,
                    dst.at[b * PER + z],
                    send.at[b * PER + d],
                    recv.at[b * PER + z],
                    x * PER + d,
                ),
            )

    def to_all(src, dst, send, recv):
        for r in (3, 2, 1, 0):
            h = pl.ds(pl.multiple_of(head_of(r) * HEAD, HEAD), HEAD)
            for d in range(PER):
                j = r * PER + d
                yield (
                    (me != j) & ((x < last_of(r)) | ((x == last_of(r)) & (z <= d))),
                    copy(src.at[:, h], dst.at[me], send.at[j], recv.at[me], j),
                )

    def wait_direct(dst, recv, b):
        for d in range(PER):
            j = b * PER + d

            @pl.when((me != j) & ((b < high) | ((b == high) & (d <= z))))
            def _():
                copy(dst.at[me], dst.at[j], recv.at[j], recv.at[j], me).wait_recv()

    def each(copies, act):
        for on, c in copies:

            @pl.when(on)
            def _():
                act(c)

    def start(c):
        c.start()

    def forward(dst, send_z, recv):
        for b in range(PER):

            @pl.when((x != b) & (b <= high))
            def _():
                copy(
                    dst.at[me], dst.at[b * PER + z], send_z.at[0], recv.at[b * PER + z], me
                ).wait_recv()
                each(along_z(dst.at[b * PER + z], dst, send_z, recv, b), start)

    def wait_row(dst, recv, b):
        for d in range(PER):

            @pl.when((z != d) & ((b < high) | ((b == high) & (d < z))))
            def _():
                copy(
                    dst.at[me], dst.at[b * PER + d], recv.at[b * PER + d], recv.at[b * PER + d], me
                ).wait_recv()

    def q_copy(src, dst, sem):
        return copy(src.at[:, q_other], dst.at[mine], sem.at[0], sem.at[1], partner)

    each(along_x(lv, v_all, v_send_x, v_recv), start)
    each(to_all(lk, k_all, k_send_z, k_recv), start)
    q_copy(lq, q_in, q_sem).start()
    q_copy(ldo, do_in, do_sem).start()
    each(along_z(lv.at[:, kv_mine], v_all, v_send_z, v_recv, x), start)

    for i in (0, 1):
        loads[i].wait()
    forward(v_all, v_send_z, v_recv)

    def spread(src, dst, p):
        for g in range(GROUP):
            dst[p, g * LONG : (g + 1) * LONG] = src[p, :, g * HEAD : (g + 1) * HEAD]

    offset = lax.broadcasted_iota(jnp.int32, (CHUNK, ROWS), 0) - lax.rem(
        lax.broadcasted_iota(jnp.int32, (CHUNK, ROWS), 1), LONG
    )
    def by_count(p, act):
        for n in range(1 + p, PER + p):

            @pl.when((low, high)[p] == n - 1)
            def _():
                act(p, n)

    def by_pair(act):
        for few, many in ((1, 4), (2, 3), (1, 2), (3, 4)):

            @pl.when((low == few - 1) & (high == many - 1))
            def _():
                act(few, many)

    def keys_of(ref, c, n=1):
        return ref[c * PER : (c + n) * PER].reshape(n * CHUNK, HEAD)

    def scores(p, n):
        tops = []
        sums = []
        for c in range(n):
            s = nt(keys_of(k_all, c), q_s[p])
            if c == n - 1:
                s = jnp.where(offset <= z * LONG, s, NEG)
            m = jnp.max(s, axis=0, keepdims=True)
            e = jnp.exp2((s - m) * SCALE2)
            e_s[p, c] = e
            tops.append(m)
            sums.append(jnp.sum(e, axis=0, keepdims=True))
        top = tops[0]
        for m in tops[1:]:
            top = jnp.maximum(top, m)
        factors = [jnp.exp2((m - top) * SCALE2) for m in tops]
        total = factors[0] * sums[0]
        for c in range(1, n):
            total = total + factors[c] * sums[c]
        inverse = 1.0 / total
        for c in range(n):
            w_s[p, c] = factors[c] * inverse

    def grad_copy(src, dst, send, recv, b, d):
        j = b * PER + d
        return copy(src.at[j], dst.at[me], send.at[j], recv.at[me], j)

    def is_sent(b, d):
        return (me != b * PER + d) & ((b < high) | ((b == high) & (d <= z)))

    def send_chunk(total, src, dst, send, recv, b):
        part = total.astype(jnp.bfloat16).reshape(PER, LONG, HEAD)
        src[pl.ds(b * PER, PER)] = part
        for d in range(PER):

            @pl.when(is_sent(b, d))
            def _():
                grad_copy(src, dst, send, recv, b, d).start()

    def shares(product, dst, few, many):
        for c in range(many):
            total = product(1, c)
            if c < few:
                total = total + product(0, c)
            send_chunk(total, *dst, c)

    def value_product(p, c):
        return nn((e_s[p, c] * w_s[p, c]).astype(jnp.bfloat16), do_s[p])

    def key_product(p, c):
        gs = (e_s[p, c] * (w_s[p, c] * (gp_s[p, c] - d_s[p]))).astype(jnp.bfloat16)
        gs_s[p, c] = gs
        return nn(gs, q_s[p]) * SCALE

    def prob_grads(p, n):
        delta = jnp.zeros((1, ROWS), jnp.float32)
        for c in range(n):
            gp = nt(keys_of(v_all, c), do_s[p])
            gp_s[p, c] = gp
            delta = delta + w_s[p, c] * jnp.sum(e_s[p, c] * gp, axis=0, keepdims=True)
        d_s[p] = delta

    def query_grads(p, n):
        gs = gs_s[p, :n].reshape(n * CHUNK, ROWS)
        return (tn(gs, keys_of(k_all, 0, n)) * SCALE).astype(jnp.bfloat16)

    dv_ends = (dv_out, dv_in, dv_send, dv_recv)
    dk_ends = (dk_out, dk_in, dk_send, dk_recv)
    loads[7].wait()
    spread(q_in, q_s, mine)
    loads[8].wait()
    spread(do_in, do_s, mine)
    q_copy(lq, q_in, q_sem).wait_recv()
    spread(q_in, q_s, other)
    for b in range(PER):
        wait_direct(k_all, k_recv, b)

    def both_scores(few, many):
        scores(0, few)
        scores(1, many)

    by_pair(both_scores)
    q_copy(ldo, do_in, do_sem).wait_recv()
    spread(do_in, do_s, other)
    by_pair(functools.partial(shares, value_product, dv_ends))
    for b in range(PER):
        wait_row(v_all, v_recv, b)

    def both_key_grads(few, many):
        prob_grads(0, few)
        prob_grads(1, many)
        shares(key_product, dk_ends, few, many)

    by_pair(both_key_grads)

    def store_query_grads(p, n):
        grad = query_grads(p, n)
        for g in range(GROUP):
            dq_out[p, :, g * HEAD : (g + 1) * HEAD] = grad[g * LONG : (g + 1) * LONG]

    dq_copy = copy(dq_out.at[other], dq_in, dq_sem.at[0], dq_sem.at[1], partner)
    for p in range(KV):
        by_count(p, store_query_grads)
        pl.when(other == p)(dq_copy.start)
    for h in range(KV):

        @pl.when(mine == h)
        def _():
            dq_o[:, h * QW : (h + 1) * QW] = dq_out[mine]

    for i in (2, 3, 4, 5, 6):
        loads[i].wait()
    ends = []
    total = jnp.int32(0)
    for i in range(DOCS):
        total = total + lens[0, 0, i]
        ends.append(total)
    outs = []
    for seg in range(SHORT // SEG):
        base = seg * SEG
        key_pos = base + lax.broadcasted_iota(jnp.int32, (SEG, GROUP * SEG), 0)
        query_pos = base + lax.rem(
            lax.broadcasted_iota(jnp.int32, (SEG, GROUP * SEG), 1), SEG
        )
        key_doc = jnp.zeros((SEG, GROUP * SEG), jnp.int32)
        query_doc = jnp.zeros((SEG, GROUP * SEG), jnp.int32)
        for end in ends:
            key_doc = key_doc + (key_pos >= end).astype(jnp.int32)
            query_doc = query_doc + (query_pos >= end).astype(jnp.int32)
        allowed = (key_doc == query_doc) & (key_pos <= query_pos)
        rows = slice(base, base + SEG)
        for h in range(KV):
            kv = slice(h * HEAD, (h + 1) * HEAD)
            cols = [
                slice((h * GROUP + g) * HEAD, (h * GROUP + g + 1) * HEAD)
                for g in range(GROUP)
            ]
            q = jnp.concatenate([sq_in[rows, c] for c in cols], axis=0)
            do = jnp.concatenate([sdo_in[rows, c] for c in cols], axis=0)
            k = sk_in[rows, kv]
            v = sv_in[rows, kv]
            s = jnp.where(allowed, nt(k, q), NEG)
            e = jnp.exp2((s - jnp.max(s, axis=0, keepdims=True)) * SCALE2)
            p = e * (1.0 / jnp.sum(e, axis=0, keepdims=True))
            gp = nt(v, do)
            delta = jnp.sum(p * gp, axis=0, keepdims=True)
            gs = (p * (gp - delta)).astype(jnp.bfloat16)
            sdv_o[rows, kv] = nn(p.astype(jnp.bfloat16), do).astype(jnp.bfloat16)
            sdk_o[rows, kv] = (nn(gs, q) * SCALE).astype(jnp.bfloat16)
            dq = (tn(gs, k) * SCALE).astype(jnp.bfloat16)
            for g, c in enumerate(cols):
                sdq_o[rows, c] = dq[g * SEG : (g + 1) * SEG]

    def wait_send(c):
        c.wait_send()

    each(to_all(lk, k_all, k_send_z, k_recv), wait_send)
    each(along_x(lv, v_all, v_send_x, v_recv), wait_send)
    for b in range(PER):
        each(along_z(v_all.at[b * PER + z], v_all, v_send_z, v_recv, b), wait_send)
        for d in range(PER):

            @pl.when(is_sent(b, d))
            def _():
                grad_copy(dv_out, dv_in, dv_send, dv_recv, b, d).wait_send()
                grad_copy(dk_out, dk_in, dk_send, dk_recv, b, d).wait_send()

    q_copy(lq, q_in, q_sem).wait_send()
    q_copy(ldo, do_in, do_sem).wait_send()
    dq_copy.wait_send()

    def sums(src, dst, recv, out):
        for h in range(KV):
            kv = slice(h * HEAD, (h + 1) * HEAD)

            @pl.when(mine == h)
            def _():
                acc_s[0] = src[me].astype(jnp.float32)

            @pl.when(mine != h)
            def _():
                acc_s[0] = jnp.zeros((LONG, HEAD), jnp.float32)

            for i in range(2):
                r = jnp.where(crossed, 2 * h + i, 2 * i + h)
                last = last_of(r)
                for d in range(PER):
                    j = r * PER + d

                    @pl.when((me != j) & ((x < last) | ((x == last) & (z <= d))))
                    def _():
                        copy(src.at[me], dst.at[j], recv.at[j], recv.at[j], me).wait_recv()
                        acc_s[0] += dst[j].astype(jnp.float32)

            out[:, kv] = acc_s[0].astype(jnp.bfloat16)

    sums(dv_out, dv_in, dv_recv, dv_o)
    sums(dk_out, dk_in, dk_recv, dk_o)
    dq_copy.wait_recv()
    for h in range(KV):

        @pl.when(mine != h)
        def _():
            dq_o[:, h * QW : (h + 1) * QW] = dq_in[...]


def write_results(*refs):
    sem = refs[12]
    copies = [pltpu.make_async_copy(refs[i], refs[6 + i], sem.at[i]) for i in range(6)]
    for copy in copies:
        copy.start()
    for copy in copies:
        copy.wait()


def on_device(lq, lk, lv, ldo, sq, sk, sv, sdo, lens):
    bf, f32 = jnp.bfloat16, jnp.float32
    args = (lq[0], lk[0], lv[0], ldo[0], sq[0], sk[0], sv[0], sdo[0], lens)
    kv, qw = KV * HEAD, KV * GROUP * HEAD
    shapes = [(LONG, qw), (LONG, kv), (LONG, kv), (SHORT, qw), (SHORT, kv), (SHORT, kv)]
    any_spec = pl.BlockSpec(memory_space=pltpu.HBM)
    vmem_spec = pl.BlockSpec(memory_space=pltpu.VMEM)
    outs = pl.pallas_call(
        kernel,
        out_shape=[pltpu.VMEM(s, bf) for s in shapes],
        in_specs=[any_spec] * 9,
        out_specs=[vmem_spec] * 6,
        scratch_shapes=[
            pltpu.VMEM((SHORT, qw), bf),
            pltpu.VMEM((SHORT, kv), bf),
            pltpu.VMEM((SHORT, kv), bf),
            pltpu.VMEM((SHORT, qw), bf),
            pltpu.VMEM((KV, LONG, QW), bf),
            pltpu.VMEM((KV, LONG, QW), bf),
            pltpu.VMEM((KV, ROWS, HEAD), bf),
            pltpu.VMEM((KV, ROWS, HEAD), bf),
            pltpu.VMEM((N, LONG, HEAD), bf),
            pltpu.VMEM((N, LONG, HEAD), bf),
            pltpu.VMEM((KV, PER, CHUNK, ROWS), f32),
            pltpu.VMEM((KV, PER, CHUNK, ROWS), f32),
            pltpu.VMEM((KV, PER, CHUNK, ROWS), bf),
            pltpu.VMEM((KV, PER, 1, ROWS), f32),
            pltpu.VMEM((KV, 1, ROWS), f32),
            pltpu.VMEM((1, LONG, HEAD), f32),
            pltpu.VMEM((N, LONG, HEAD), bf),
            pltpu.VMEM((N, LONG, HEAD), bf),
            pltpu.VMEM((N, LONG, HEAD), bf),
            pltpu.VMEM((N, LONG, HEAD), bf),
            pltpu.VMEM((KV, LONG, QW), bf),
            pltpu.VMEM((LONG, QW), bf),
            pltpu.SMEM((1, 1, DOCS), jnp.int32),
            pltpu.SemaphoreType.DMA((9,)),
        ]
        + [pltpu.SemaphoreType.DMA((n,)) for n in (PER, N, N) * 2 + (N,) * 4 + (2,) * 3],
        compiler_params=pltpu.CompilerParams(
            collective_id=0, has_side_effects=True, vmem_limit_bytes=40 << 20
        ),
        name="attention_grads",
    )(*(pltpu.with_memory_space_constraint(a, pltpu.HBM) for a in args))
    outs = pl.pallas_call(
        write_results,
        out_shape=[jax.ShapeDtypeStruct(s, bf) for s in shapes],
        in_specs=[vmem_spec] * 6,
        out_specs=[any_spec] * 6,
        scratch_shapes=[pltpu.SemaphoreType.DMA((6,))],
        compiler_params=pltpu.CompilerParams(vmem_limit_bytes=1 << 20),
        name="write_results",
    )(*(pltpu.with_memory_space_constraint(o, pltpu.VMEM) for o in outs))
    return tuple(o[None] for o in outs)


def solution(mesh):
    spec = P("dp", "context", "head")
    return jax.shard_map(
        on_device,
        mesh=mesh,
        in_specs=(spec,) * 8 + (P("dp", "context", None),),
        out_specs=(spec,) * 6,
        check_vma=False,
    )
```
